1024 devices in a mesh: owner: 64 (over x, z), dp: 16 (over y, core).
Axes of the slice: x: 8, y: 8, z: 8, core: 2. Of those that a mesh axis runs over, the one named last changes fastest.
Arguments:
- grads: bfloat16 [16, 48, 16, 64, 1024], P('dp', None, None, 'owner'), may hold values from -6 to 6
- owner_map: int32 [48], replicated, may hold values from 0 to 63, as said below
- block_dims: int32 [48, 2], replicated, may hold values from 1 to 8
- left_root: bfloat16 [64, 2, 1024, 1024], P('owner'), may hold values from -0.3 to 2, as said below
- right_root: bfloat16 [64, 2, 1024, 1024], P('owner'), may hold values from -0.3 to 2, as said below
Outputs:
- direction: bfloat16 [48, 16, 64, 1024], P(None, 'dp', 'owner')
The draws below stay inside these ranges and needn't reach their ends.
Inputs may be any that keep to these rules, and one draw needn't show every extreme that they name: `owner_map`: every owner column owns 0, 1 or 2 blocks, and some column owns exactly 2. `left_root`: each matrix is symmetric. `right_root`: each matrix is symmetric.
All inputs are finite; a program needn't handle non-finite values.
Results may differ from the reference program's by a relative error of at most 0.0057.
Values may be sent and summed in bfloat16 or wider, within the bound.
A program may use at most 32 MiB of HBM per device.

```python
import math
import jax
import jax.numpy as jnp
from jax import lax

BS = 1024
CAP = 2
BLOCKS = 48
TILE = 128
PIECE = 1024
N_OWNER = 64
N_DP = 16


def draw_owner_map(key, part):
    key = jax.random.fold_in(key, 11)
    first_key, second_key, third_key = jax.random.split(key, 3)
    busy_count = jax.random.randint(first_key, (), N_OWNER // 8, N_OWNER // 4 + 1)
    position = jnp.arange(BLOCKS) // (CAP // 2)
    rank = jnp.where(position < 2 * busy_count, position // 2, busy_count + position - 2 * busy_count)
    owner_order = jax.random.permutation(second_key, N_OWNER)
    placed = owner_order[rank]
    block_order = jax.random.permutation(third_key, BLOCKS)
    return placed[block_order].astype(jnp.int32)


def symmetric_root(diagonal, noise):
    identity = jnp.eye(BS, dtype=jnp.float32)
    paired = 0.5 * (noise + jnp.swapaxes(noise, -1, -2))
    return identity * diagonal[..., None, :] + paired * (1.0 - identity)


def draw_left_root(key, part):
    key = jax.random.fold_in(key, 21)
    first_key, second_key = jax.random.split(key)
    spread = 0.8 / math.sqrt(BS)
    diagonal = jnp.exp(jax.random.uniform(first_key, (N_OWNER, CAP, BS), jnp.float32, math.log(0.2), math.log(2.0)))
    noise = jnp.clip(spread * jax.random.normal(second_key, (N_OWNER, CAP, BS, BS), jnp.float32), -3.0 * spread, 3.0 * spread)
    return symmetric_root(diagonal, noise).astype(jnp.bfloat16)


def draw_right_root(key, part):
    key = jax.random.fold_in(key, 37)
    first_key, second_key = jax.random.split(key)
    spread = 0.8 / math.sqrt(BS)
    diagonal = jnp.exp(jax.random.uniform(first_key, (N_OWNER, CAP, BS), jnp.float32, math.log(0.2), math.log(2.0)))
    noise = jnp.clip(spread * jax.random.normal(second_key, (N_OWNER, CAP, BS, BS), jnp.float32), -3.0 * spread, 3.0 * spread)
    return symmetric_root(diagonal, noise).astype(jnp.bfloat16)


def place_ends(drawn, stream_key, low, top_value):
    dims = drawn.shape
    place = [jax.random.randint(jax.random.fold_in(stream_key, axis), (), 0, dims[axis]) for axis in range(len(dims))]
    drawn = drawn.at[tuple(place)].set(low)
    longest = dims.index(max(dims))
    place[longest] = (place[longest] + 1) % dims[longest]
    return drawn.at[tuple(place)].set(top_value)


def with_spikes(values, stream_key, source, target, blocks, factor):
    def block_of(axis_at):
        return (jnp.arange(values.shape[axis_at]) // (values.shape[axis_at] // blocks)).reshape((-1,) + (1,) * (values.ndim - 1 - axis_at))

    near = jax.random.permutation(stream_key, blocks)[block_of(target)]
    other_side = (block_of(target) + blocks // 2) % blocks
    return jnp.where((block_of(source) == near) | (block_of(source) == other_side), factor * values, values)


def levels(rng, shape, shards, least, largest):
    def one(dim, parts):
        heights = jax.random.uniform(jax.random.fold_in(jax.random.fold_in(rng, 6), dim), (parts,), jnp.float32, least / len(shards), largest / len(shards))
        return jnp.repeat(jnp.exp(heights), shape[dim] // parts).reshape((-1,) + (1,) * (len(shape) - dim - 1))

    gain = one(*shards[0])
    for cut in shards[1:]:
        gain = gain * one(*cut)
    return gain


def heavy_noise(rng, shape, scale, limit, pieces, heavy, kind=jnp.bfloat16):
    array = scale * jax.random.normal(rng, shape, jnp.float32)
    if pieces:
        array = array * levels(rng, shape, pieces, -0.22, 0.18)
    return jnp.clip(with_spikes(array, jax.random.fold_in(rng, 3), *heavy), -limit, limit).astype(kind)


def setup_inputs(seed: int = 0) -> dict:
    splits = jax.random.split(jax.random.key(seed), 6)
    return {
        "grads": heavy_noise(splits[0], (N_DP, BLOCKS, N_DP, N_OWNER, PIECE), 1.0, 6.0, ((0, 16), (3, 64)), (0, 2, 16, 2.0)),
        "owner_map": draw_owner_map(jax.random.fold_in(splits[5], 71), 0),
        "block_dims": place_ends(jax.random.randint(splits[2], (BLOCKS, 2), 1, 9), jax.random.fold_in(splits[2], 1), 1, 8).astype(jnp.int32),
        "left_root": draw_left_root(jax.random.fold_in(splits[5], 71), 0),
        "right_root": draw_right_root(jax.random.fold_in(splits[5], 71), 0),
    }


def owner_slots(owner_map):
    block_count = owner_map.shape[0]
    same_owner = owner_map[:, None] == owner_map[None, :]
    earlier = jnp.arange(block_count)[None, :] < jnp.arange(block_count)[:, None]
    return jnp.sum((same_owner & earlier).astype(jnp.int32), axis=1).astype(jnp.int32)


def reference(grads, owner_map, block_dims, left_root, right_root):
    summed = jnp.sum(grads, axis=0, dtype=jnp.float32).astype(jnp.bfloat16)
    matrices = summed.reshape(BLOCKS, BS, BS)
    slot_of = owner_slots(owner_map)
    row_ids = jnp.arange(BS).astype(jnp.int32)

    def one_block(block_id):
        owner_id = owner_map[block_id]
        slot_id = slot_of[block_id]
        live_rows = block_dims[block_id, 0] * TILE
        live_cols = block_dims[block_id, 1] * TILE
        live_mask = (row_ids[:, None] < live_rows) & (row_ids[None, :] < live_cols)
        masked = jnp.where(live_mask, matrices[block_id], jnp.zeros((), matrices.dtype))
        left_full = left_root[owner_id, slot_id]
        right_full = right_root[owner_id, slot_id]
        product = jnp.dot(left_full, masked, preferred_element_type=jnp.float32).astype(jnp.bfloat16)
        update = jnp.dot(product, right_full, preferred_element_type=jnp.float32)
        return jnp.where(live_mask, update, jnp.zeros((), jnp.float32)).astype(jnp.bfloat16)

    result = lax.map(one_block, jnp.arange(BLOCKS).astype(jnp.int32))
    return result.reshape(BLOCKS, N_DP, N_OWNER, PIECE)
```

```python
import functools

import jax
import jax.numpy as jnp
from jax import lax
from jax.experimental import pallas as pl
from jax.experimental.pallas import tpu as pltpu
from jax.sharding import PartitionSpec as P

MESH = pl.DeviceIdType.MESH
F32, BF16, I32 = jnp.float32, jnp.bfloat16, jnp.int32
NB = 48
HALF = NB // 2
NO = 64
NY = 8
LANES = 128
FAR_FIRST = (4, 3, 5, 2, 6, 1, 7)


def remote(src, dst, send_sem, recv_sem, owner, dp):
    return pltpu.make_async_remote_copy(
        src_ref=src, dst_ref=dst, send_sem=send_sem, recv_sem=recv_sem,
        device_id={"owner": owner, "dp": dp}, device_id_type=MESH,
    )


def signal(sem, owner, dp):
    pl.semaphore_signal(sem, inc=1, device_id={"owner": owner, "dp": dp}, device_id_type=MESH)


def diagonal_column(row):
    sub = lax.broadcasted_iota(I32, (LANES, LANES), 0)
    lane = lax.broadcasted_iota(I32, (LANES, LANES), 1)
    return jnp.sum(jnp.where(sub == lane, row, 0), axis=1, keepdims=True)


def build_tables(map_ref, dims_ref, rows, table):
    rows[...] = jnp.full((8, LANES), -1, I32)
    rows[0:1, 0:NB] = map_ref[...]
    rows[1:3, 0:NB] = dims_ref[...]
    sub = lax.broadcasted_iota(I32, (LANES, LANES), 0)
    lane = lax.broadcasted_iota(I32, (LANES, LANES), 1)
    owner_row = rows[0:1, :]
    owner_col = diagonal_column(owner_row)
    live_rows = diagonal_column(rows[1:2, :])
    live_cols = diagonal_column(rows[2:3, :])
    same = owner_col == owner_row
    slot_row = jnp.sum(jnp.where(same & (sub < lane), 1, 0), axis=0, keepdims=True)
    slot_col = jnp.sum(jnp.where(same & (lane < sub), 1, 0), axis=1, keepdims=True)
    owned = owner_col == lane
    for slot in range(2):
        hit = owned & (slot_col == slot)
        for row, value in ((slot, sub), (2 + slot, live_rows), (4 + slot, live_cols)):
            table[row : row + 1, :] = jnp.sum(jnp.where(hit, value, 0), axis=0, keepdims=True)
    table[6:7, :] = owner_row
    table[7:8, :] = slot_row


def kernel(
    grads, map_ref, dims_ref, left, right, out_ref,
    g, gin, pair, rsin, red, out1, in1, lv, rv, g32, prod, pin, dsc, xin, y32, out2, in2, f32s, rows, table, tab,
    load_sem, core_s, core_r, rs_s, rs_r, red_s, red_r, a1_s, a1_r, e_s, e_r, x_s, x_r, a2_s, a2_r,
):
    me = lax.axis_index("owner")
    dp = lax.axis_index("dp")
    x, z = lax.div(me, 8), lax.rem(me, 8)
    y, c = lax.div(dp, 2), lax.rem(dp, 2)
    other = dp + 1 - 2 * c

    load_g = pltpu.make_async_copy(grads, g, load_sem.at[0])
    load_l = pltpu.make_async_copy(left.at[c], lv, load_sem.at[1])
    load_r = pltpu.make_async_copy(right.at[c], rv, load_sem.at[2])
    load_g.start()

    def owner_at(i):
        return lax.rem(x + lax.rem(i, 8), 8) * 8 + lax.rem(z + lax.div(i, 8), 8)

    def dp_at(offset):
        return lax.rem(y + offset, NY)

    barrier = pltpu.get_barrier_semaphore()
    signal(barrier, me, other)
    for offset in FAR_FIRST:
        signal(barrier, me, dp_at(offset) * 2 + c)

    def greet(i, carry):
        signal(barrier, owner_at(i), dp)
        return carry

    lax.fori_loop(1, NO, greet, 0)
    pl.semaphore_wait(barrier, 1 + 7 + NO - 1)

    mine, theirs = c * HALF, (1 - c) * HALF
    load_g.wait()
    halves = []
    for i, offset in enumerate(FAR_FIRST + (0,)):
        tile = pl.ds(pl.multiple_of(dp_at(offset) * LANES, LANES), LANES)
        copy = remote(g.at[pl.ds(theirs, HALF), :, tile], gin.at[i], core_s.at[i], core_r.at[i], me, other)
        copy.start()
        halves.append((copy, tile))
    load_l.start()
    load_r.start()
    sends = []
    for i, offset in enumerate(FAR_FIRST):
        copy, tile = halves[i]
        copy.wait_recv()

        def add(b, carry, i=i, tile=tile):
            pair[i, b] = (g[mine + b, :, tile].astype(F32) + gin[i, b].astype(F32)).astype(BF16)
            return carry

        lax.fori_loop(0, HALF, add, 0, unroll=4)
        send = remote(pair.at[i], rsin.at[i], rs_s.at[i], rs_r.at[i], me, dp_at(offset) * 2 + c)
        send.start()
        sends.append(send)

    build_tables(map_ref, dims_ref, rows, table)
    to_scalars = pltpu.make_async_copy(table, tab, load_sem.at[3])
    to_scalars.start()
    to_scalars.wait()

    own_copy, own_tile = halves[7]
    own_copy.wait_recv()
    for send in sends:
        send.wait_recv()

    def total(b, carry):
        acc = g[mine + b, :, own_tile].astype(F32) + gin[7, b].astype(F32)
        for i in range(7):
            acc = acc + rsin[i, b].astype(F32)
        red[mine + b] = acc.astype(BF16)
        return carry

    lax.fori_loop(0, HALF, total, 0, unroll=2)
    share = remote(red.at[pl.ds(mine, HALF)], red.at[pl.ds(mine, HALF)], red_s, red_r, me, other)
    share.start()
    share.wait_recv()

    def block_at(t):
        return jnp.clip(tab[c, t], 0, NB - 1)

    in1[me] = red[block_at(me)]

    def dispatch(i, carry):
        t = owner_at(i)
        out1[t] = red[block_at(t)]
        remote(out1.at[t], in1.at[me], a1_s, a1_r, t, dp).start()
        return carry

    lax.fori_loop(1, NO, dispatch, 0)
    load_l.wait()
    pltpu.make_async_copy(out1.at[pl.ds(0, NO - 1)], in1.at[pl.ds(0, NO - 1)], a1_r).wait()

    live_rows, live_cols = tab[2 + c, me], tab[4 + c, me]
    in_columns = jnp.where(y < live_cols, 1, 0)
    row_limit = live_rows * 2 * in_columns

    def place(q, carry):
        tile = in1[q].astype(F32)
        keep = lax.broadcasted_iota(I32, (16, LANES), 0) < row_limit
        g32[pl.ds(q, 16, stride=NO), :] = jnp.where(keep, tile, 0.0)
        return carry

    lax.fori_loop(0, NO, place, 0, unroll=4)
    product = jnp.dot(lv[...], g32[pl.ds(0, 8 * LANES), :].astype(BF16), preferred_element_type=F32).astype(BF16)
    prod[...] = product.reshape(NY, LANES, LANES)

    my_tile = pl.ds(pl.multiple_of(y * LANES, LANES), LANES)
    bands = []
    for i, offset in enumerate(FAR_FIRST):
        t = dp_at(offset)
        copy = remote(prod.at[t], pin.at[:, my_tile], e_s.at[i], e_r.at[i], me, t * 2 + c)
        copy.start()
        bands.append(copy)
    pin[:, my_tile] = prod[y]
    load_r.wait()
    for copy in bands:
        copy.wait_recv()
    update = jnp.dot(pin[...], rv[...], preferred_element_type=F32)
    column_limit = live_cols * LANES * jnp.where(y < live_rows, 1, 0)
    keep = lax.broadcasted_iota(I32, (LANES, 8 * LANES), 1) < column_limit
    update = jnp.where(keep, update, 0.0).astype(BF16)
    for half in range(2):
        for j in range(8):
            dsc[half, j] = update[half * NO : (half + 1) * NO, j * LANES : (j + 1) * LANES]
    swap = remote(dsc.at[1 - c], xin, x_s, x_r, me, other)
    swap.start()
    for j in range(8):
        y32[pl.ds(c * 8 + j, NO, stride=16), :] = dsc[c, j].astype(F32)
    swap.wait_recv()
    for j in range(8):
        y32[pl.ds((1 - c) * 8 + j, NO, stride=16), :] = xin[j].astype(F32)
    out2[...] = y32[pl.ds(0, NO * 16), :].astype(BF16).reshape(NO, 16, LANES)

    in2[me] = out2[me]

    def give_back(i, carry):
        t = owner_at(i)
        remote(out2.at[t], in2.at[me], a2_s, a2_r, t, dp).start()
        return carry

    lax.fori_loop(1, NO, give_back, 0)
    pltpu.make_async_copy(out2.at[pl.ds(0, NO - 1)], in2.at[pl.ds(0, NO - 1)], a2_r).wait()

    def pick(b, carry):
        both = in2[jnp.clip(tab[6, b], 0, NO - 1)].astype(F32)
        first = jnp.where(tab[7, b] == 0, 1, 0)
        chosen = jnp.where(first == 1, both[:8], both[8:])
        f32s[pl.ds(pl.multiple_of(b * 8, 8), 8), :] = chosen
        return carry

    lax.fori_loop(0, NB, pick, 0, unroll=4)
    for j in range(8):
        out_ref[:, j * LANES : (j + 1) * LANES] = f32s[pl.ds(j, NB, stride=8), :].astype(BF16)

    for copy, _ in halves:
        copy.wait_send()
    for copy in sends:
        copy.wait_send()
    share.wait_send()
    pltpu.make_async_copy(out1.at[pl.ds(0, NO - 1)], in1.at[pl.ds(0, NO - 1)], a1_s).wait()
    for copy in bands:
        copy.wait_send()
    swap.wait_send()
    pltpu.make_async_copy(out2.at[pl.ds(0, NO - 1)], in2.at[pl.ds(0, NO - 1)], a2_s).wait()


def on_device(grads, owner_map, block_dims, left_root, right_root):
    any_spec = pl.BlockSpec(memory_space=pltpu.HBM)
    vmem_spec = pl.BlockSpec(memory_space=pltpu.VMEM)
    dma = pltpu.SemaphoreType.DMA
    out = pl.pallas_call(
        kernel,
        out_shape=jax.ShapeDtypeStruct((NB, 8 * LANES), BF16),
        in_specs=[any_spec, vmem_spec, vmem_spec, any_spec, any_spec],
        out_specs=vmem_spec,
        scratch_shapes=[
            pltpu.VMEM((NB, 16, 8 * LANES), BF16),
            pltpu.VMEM((8, HALF, 16, LANES), BF16),
            pltpu.VMEM((7, HALF, 16, LANES), BF16),
            pltpu.VMEM((7, HALF, 16, LANES), BF16),
            pltpu.VMEM((NB, 16, LANES), BF16),
            pltpu.VMEM((NO, 16, LANES), BF16),
            pltpu.VMEM((NO, 16, LANES), BF16),
            pltpu.VMEM((8 * LANES, 8 * LANES), BF16),
            pltpu.VMEM((8 * LANES, 8 * LANES), BF16),
            pltpu.VMEM((8 * LANES + NO, LANES), F32),
            pltpu.VMEM((NY, LANES, LANES), BF16),
            pltpu.VMEM((LANES, 8 * LANES), BF16),
            pltpu.VMEM((2, 8, NO, LANES), BF16),
            pltpu.VMEM((8, NO, LANES), BF16),
            pltpu.VMEM((NO * 16 + 16, LANES), F32),
            pltpu.VMEM((NO, 16, LANES), BF16),
            pltpu.VMEM((NO, 16, LANES), BF16),
            pltpu.VMEM((NB * 8 + 8, LANES), F32),
            pltpu.VMEM((8, LANES), I32),
            pltpu.VMEM((8, LANES), I32),
            pltpu.SMEM((8, LANES), I32),
            dma((4,)),
            dma((8,)), dma((8,)),
            dma((7,)), dma((7,)),
            dma, dma,
            dma, dma,
            dma((7,)), dma((7,)),
            dma, dma,
            dma, dma,
        ],
        compiler_params=pltpu.CompilerParams(
            collective_id=0, has_side_effects=True, vmem_limit_bytes=60 * 1024 * 1024
        ),
    )(
        grads.reshape(NB, 16, 8 * LANES),
        owner_map.reshape(1, NB),
        block_dims.T,
        left_root[0],
        right_root[0],
    )
    return out.reshape(NB, 1, 1, 8 * LANES)


def solution(mesh):
    placed = (
        P("dp", None, None, "owner", None),
        P(),
        P(),
        P("owner", None, None, None),
        P("owner", None, None, None),
    )
    return jax.shard_map(
        on_device,
        mesh=mesh,
        in_specs=placed,
        out_specs=P(None, "dp", "owner", None),
        check_vma=False,
    )
```

```python
import functools

import jax
import jax.numpy as jnp
from jax import lax
from jax.experimental import pallas as pl
from jax.experimental.pallas import tpu as pltpu
from jax.sharding import PartitionSpec as P

MESH = pl.DeviceIdType.MESH
F32, BF16, I32 = jnp.float32, jnp.bfloat16, jnp.int32
NB = 48
HALF = NB // 2
QUARTER = HALF // 2
NO = 64
NY = 8
LANES = 128
FAR_FIRST = (4, 3, 5, 2, 6, 1, 7)
TILE_ORDER = (4, 3, 5, 1, 7, 2, 6, 0)


def remote(src, dst, send_sem, recv_sem, owner, dp):
    return pltpu.make_async_remote_copy(
        src_ref=src, dst_ref=dst, send_sem=send_sem, recv_sem=recv_sem,
        device_id={"owner": owner, "dp": dp}, device_id_type=MESH,
    )


def signal(sem, owner, dp):
    pl.semaphore_signal(sem, inc=1, device_id={"owner": owner, "dp": dp}, device_id_type=MESH)


def diagonal_column(row):
    sub = lax.broadcasted_iota(I32, (LANES, LANES), 0)
    lane = lax.broadcasted_iota(I32, (LANES, LANES), 1)
    return jnp.sum(jnp.where(sub == lane, row, 0), axis=1, keepdims=True)


def build_tables(map_ref, dims_ref, rows, table):
    rows[...] = jnp.full((8, LANES), -1, I32)
    rows[0:1, 0:NB] = map_ref[...]
    rows[1:3, 0:NB] = dims_ref[...]
    sub = lax.broadcasted_iota(I32, (LANES, LANES), 0)
    lane = lax.broadcasted_iota(I32, (LANES, LANES), 1)
    owner_row = rows[0:1, :]
    owner_col = diagonal_column(owner_row)
    live_rows = diagonal_column(rows[1:2, :])
    live_cols = diagonal_column(rows[2:3, :])
    same = owner_col == owner_row
    slot_row = jnp.sum(jnp.where(same & (sub < lane), 1, 0), axis=0, keepdims=True)
    slot_col = jnp.sum(jnp.where(same & (lane < sub), 1, 0), axis=1, keepdims=True)
    owned = owner_col == lane
    for slot in range(2):
        hit = owned & (slot_col == slot)
        for row, value in ((slot, sub), (2 + slot, live_rows), (4 + slot, live_cols)):
            table[row : row + 1, :] = jnp.sum(jnp.where(hit, value, 0), axis=0, keepdims=True)
    table[6:7, :] = owner_row
    table[7:8, :] = slot_row


def kernel(
    grads, map_ref, dims_ref, left, right, out_ref,
    g, gin, pair, far, mid, near, relayed, red, out1, in1, lv, rv, g32, prod, pin, dsc, xin, y32, out2, in2, f32s, rows, table, tab,
    load_sem, plane, core_s, core_r, rs_s, rs_r, red_s, red_r, a1_s, a1_r, e_s, e_r, x_s, x_r, a2_s, a2_r,
):
    me = lax.axis_index("owner")
    dp = lax.axis_index("dp")
    x, z = lax.div(me, 8), lax.rem(me, 8)
    y, c = lax.div(dp, 2), lax.rem(dp, 2)
    other = dp + 1 - 2 * c

    load_g = pltpu.make_async_copy(grads, g, load_sem.at[0])
    load_l = pltpu.make_async_copy(left.at[c], lv, load_sem.at[1])
    load_r = pltpu.make_async_copy(right.at[c], rv, load_sem.at[2])
    load_g.start()

    def along_x(i):
        return lax.rem(x + i, 8) * 8 + z

    def along_z(i):
        return x * 8 + lax.rem(z + i, 8)

    def owner_at(i):
        return lax.rem(x + lax.rem(i, 8), 8) * 8 + lax.rem(z + lax.div(i, 8), 8)

    def dp_at(offset):
        return lax.rem(y + offset, NY)

    pending = []
    barrier = pltpu.get_barrier_semaphore()
    signal(barrier, me, other)
    for offset in (1, 7, 2, 6):
        signal(barrier, me, dp_at(offset) * 2 + c)
    for i in range(1, 8):
        signal(barrier, along_x(i), dp)
        signal(barrier, along_z(i), dp)
    pl.semaphore_wait(barrier, 1 + 4 + 14)

    mine, theirs = c * HALF, (1 - c) * HALF
    load_g.wait()
    halves = {}
    for offset in TILE_ORDER:
        tile = pl.ds(pl.multiple_of(dp_at(offset) * LANES, LANES), LANES)
        copy = remote(
            g.at[pl.ds(theirs, HALF), :, tile], gin.at[offset], core_s.at[offset], core_r.at[offset], me, other
        )
        copy.start()
        pending.append(copy.wait_send)
        halves[offset] = (copy, tile)
    load_l.start()
    load_r.start()

    def core_sum(offset, b):
        return g[mine + b, :, halves[offset][1]].astype(F32) + gin[offset, b].astype(F32)

    def send_sum(offset, hops):
        halves[offset][0].wait_recv()

        def add(b, carry):
            pair[offset, b] = core_sum(offset, b).astype(BF16)
            return carry

        lax.fori_loop(0, HALF, add, 0, unroll=4)
        copies = []
        for buffer, index, first, count, target, k in hops:
            copy = remote(
                pair.at[offset, pl.ds(first, count)], buffer.at[index], rs_s.at[k], rs_r.at[k], me, dp_at(target) * 2 + c
            )
            copy.start()
            pending.append(copy.wait_send)
            copies.append(copy)
        return copies

    far_up, far_down = send_sum(4, ((far, 0, 0, QUARTER, 2, 0), (far, 1, QUARTER, QUARTER, 6, 1)))
    (mid_up,) = send_sum(3, ((mid, 0, 0, HALF, 1, 2),))
    (mid_down,) = send_sum(5, ((mid, 1, 0, HALF, 7, 3),))
    (near_up,) = send_sum(1, ((near, 0, 0, HALF, 1, 4),))
    (near_down,) = send_sum(7, ((near, 1, 0, HALF, 7, 5),))
    for i in range(1, 8):
        signal(plane, along_x(i), dp)
    relays = []
    for way, offset, first, arrivals in ((0, 2, 0, (far_up, mid_up)), (1, 6, QUARTER, (far_down, mid_down))):
        halves[offset][0].wait_recv()
        for copy in arrivals:
            copy.wait_recv()

        def relay_both(b, carry, way=way, offset=offset, first=first):
            acc = core_sum(offset, first + b) + mid[way, first + b].astype(F32) + far[way, b].astype(F32)
            pair[offset, first + b] = acc.astype(BF16)
            return carry

        def relay_one(b, carry, way=way, offset=offset, first=QUARTER - first):
            pair[offset, first + b] = (core_sum(offset, first + b) + mid[way, first + b].astype(F32)).astype(BF16)
            return carry

        lax.fori_loop(0, QUARTER, relay_both, 0, unroll=4)
        lax.fori_loop(0, QUARTER, relay_one, 0, unroll=4)
        copy = remote(pair.at[offset], relayed.at[way], rs_s.at[6 + way], rs_r.at[6 + way], me, dp_at(offset) * 2 + c)
        copy.start()
        pending.append(copy.wait_send)
        relays.append(copy)

    build_tables(map_ref, dims_ref, rows, table)
    to_scalars = pltpu.make_async_copy(table, tab, load_sem.at[3])
    to_scalars.start()
    to_scalars.wait()

    halves[0][0].wait_recv()
    for copy in (near_up, near_down, *relays):
        copy.wait_recv()

    def total(b, carry):
        acc = core_sum(0, b)
        for way in range(2):
            acc = acc + near[way, b].astype(F32) + relayed[way, b].astype(F32)
        red[mine + b] = acc.astype(BF16)
        return carry

    lax.fori_loop(0, HALF, total, 0, unroll=4)
    share = remote(red.at[pl.ds(mine, HALF)], red.at[pl.ds(mine, HALF)], red_s, red_r, me, other)
    share.start()
    pending.append(share.wait_send)
    share.wait_recv()

    pl.semaphore_wait(plane, 7)

    def block_at(t):
        return jnp.clip(tab[c, t], 0, NB - 1)

    in1[me] = red[block_at(me)]

    def dispatch(i, carry):
        t = owner_at(i)
        out1[t] = red[block_at(t)]
        remote(out1.at[t], in1.at[me], a1_s, a1_r, t, dp).start()
        return carry

    lax.fori_loop(1, NO, dispatch, 0)
    pending.append(pltpu.make_async_copy(out1.at[pl.ds(0, NO - 1)], in1.at[pl.ds(0, NO - 1)], a1_s).wait)
    load_l.wait()
    pltpu.make_async_copy(out1.at[pl.ds(0, NO - 1)], in1.at[pl.ds(0, NO - 1)], a1_r).wait()

    live_rows, live_cols = tab[2 + c, me], tab[4 + c, me]
    in_columns = jnp.where(y < live_cols, 1, 0)
    row_limit = live_rows * 2 * in_columns

    def place(q, carry):
        tile = in1[q].astype(F32)
        keep = lax.broadcasted_iota(I32, (16, LANES), 0) < row_limit
        g32[pl.ds(q, 16, stride=NO), :] = jnp.where(keep, tile, 0.0)
        return carry

    lax.fori_loop(0, NO, place, 0, unroll=4)
    product = jnp.dot(lv[...], g32[pl.ds(0, 8 * LANES), :].astype(BF16), preferred_element_type=F32).astype(BF16)
    prod[...] = product.reshape(NY, LANES, LANES)

    my_tile = pl.ds(pl.multiple_of(y * LANES, LANES), LANES)
    bands = []
    for i, offset in enumerate(FAR_FIRST):
        t = dp_at(offset)
        copy = remote(prod.at[t], pin.at[:, my_tile], e_s.at[i], e_r.at[i], me, t * 2 + c)
        copy.start()
        pending.append(copy.wait_send)
        bands.append(copy)
    pin[:, my_tile] = prod[y]
    load_r.wait()
    for copy in bands:
        copy.wait_recv()
    update = jnp.dot(pin[...], rv[...], preferred_element_type=F32)
    column_limit = live_cols * LANES * jnp.where(y < live_rows, 1, 0)
    keep = lax.broadcasted_iota(I32, (LANES, 8 * LANES), 1) < column_limit
    update = jnp.where(keep, update, 0.0).astype(BF16)
    for half in range(2):
        for j in range(8):
            dsc[half, j] = update[half * NO : (half + 1) * NO, j * LANES : (j + 1) * LANES]
    swap = remote(dsc.at[1 - c], xin, x_s, x_r, me, other)
    swap.start()
    pending.append(swap.wait_send)
    for j in range(8):
        y32[pl.ds(c * 8 + j, NO, stride=16), :] = dsc[c, j].astype(F32)
    swap.wait_recv()
    for j in range(8):
        y32[pl.ds((1 - c) * 8 + j, NO, stride=16), :] = xin[j].astype(F32)
    out2[...] = y32[pl.ds(0, NO * 16), :].astype(BF16).reshape(NO, 16, LANES)

    in2[me] = out2[me]

    def give_back(i, carry):
        t = owner_at(i)
        remote(out2.at[t], in2.at[me], a2_s, a2_r, t, dp).start()
        return carry

    lax.fori_loop(1, NO, give_back, 0)
    pending.append(pltpu.make_async_copy(out2.at[pl.ds(0, NO - 1)], in2.at[pl.ds(0, NO - 1)], a2_s).wait)
    pltpu.make_async_copy(out2.at[pl.ds(0, NO - 1)], in2.at[pl.ds(0, NO - 1)], a2_r).wait()

    def pick(b, carry):
        both = in2[jnp.clip(tab[6, b], 0, NO - 1)].astype(F32)
        first = jnp.where(tab[7, b] == 0, 1, 0)
        chosen = jnp.where(first == 1, both[:8], both[8:])
        f32s[pl.ds(pl.multiple_of(b * 8, 8), 8), :] = chosen
        return carry

    lax.fori_loop(0, NB, pick, 0, unroll=4)
    for j in range(8):
        out_ref[:, j * LANES : (j + 1) * LANES] = f32s[pl.ds(j, NB, stride=8), :].astype(BF16)

    for wait in pending:
        wait()


def on_device(grads, owner_map, block_dims, left_root, right_root):
    any_spec = pl.BlockSpec(memory_space=pltpu.HBM)
    vmem_spec = pl.BlockSpec(memory_space=pltpu.VMEM)
    dma = pltpu.SemaphoreType.DMA
    out = pl.pallas_call(
        kernel,
        out_shape=jax.ShapeDtypeStruct((NB, 8 * LANES), BF16),
        in_specs=[any_spec, vmem_spec, vmem_spec, any_spec, any_spec],
        out_specs=vmem_spec,
        scratch_shapes=[
            pltpu.VMEM((NB, 16, 8 * LANES), BF16),
            pltpu.VMEM((8, HALF, 16, LANES), BF16),
            pltpu.VMEM((8, HALF, 16, LANES), BF16),
            pltpu.VMEM((2, QUARTER, 16, LANES), BF16),
            pltpu.VMEM((2, HALF, 16, LANES), BF16),
            pltpu.VMEM((2, HALF, 16, LANES), BF16),
            pltpu.VMEM((2, HALF, 16, LANES), BF16),
            pltpu.VMEM((NB, 16, LANES), BF16),
            pltpu.VMEM((NO, 16, LANES), BF16),
            pltpu.VMEM((NO, 16, LANES), BF16),
            pltpu.VMEM((8 * LANES, 8 * LANES), BF16),
            pltpu.VMEM((8 * LANES, 8 * LANES), BF16),
            pltpu.VMEM((8 * LANES + NO, LANES), F32),
            pltpu.VMEM((NY, LANES, LANES), BF16),
            pltpu.VMEM((LANES, 8 * LANES), BF16),
            pltpu.VMEM((2, 8, NO, LANES), BF16),
            pltpu.VMEM((8, NO, LANES), BF16),
            pltpu.VMEM((NO * 16 + 16, LANES), F32),
            pltpu.VMEM((NO, 16, LANES), BF16),
            pltpu.VMEM((NO, 16, LANES), BF16),
            pltpu.VMEM((NB * 8 + 8, LANES), F32),
            pltpu.VMEM((8, LANES), I32),
            pltpu.VMEM((8, LANES), I32),
            pltpu.SMEM((8, LANES), I32),
            dma((4,)),
            pltpu.SemaphoreType.REGULAR,
            dma((8,)), dma((8,)),
            dma((8,)), dma((8,)),
            dma, dma,
            dma, dma,
            dma((7,)), dma((7,)),
            dma, dma,
            dma, dma,
        ],
        compiler_params=pltpu.CompilerParams(
            collective_id=0, has_side_effects=True, vmem_limit_bytes=60 * 1024 * 1024
        ),
    )(
        grads.reshape(NB, 16, 8 * LANES),
        owner_map.reshape(1, NB),
        block_dims.T,
        left_root[0],
        right_root[0],
    )
    return out.reshape(NB, 1, 1, 8 * LANES)


def solution(mesh):
    placed = (
        P("dp", None, None, "owner", None),
        P(),
        P(),
        P("owner", None, None, None),
        P("owner", None, None, None),
    )
    return jax.shard_map(
        on_device,
        mesh=mesh,
        in_specs=placed,
        out_specs=P(None, "dp", "owner", None),
        check_vma=False,
    )
```

```python
import functools

import jax
import jax.numpy as jnp
from jax import lax
from jax.experimental import pallas as pl
from jax.experimental.pallas import tpu as pltpu
from jax.sharding import PartitionSpec as P

MESH = pl.DeviceIdType.MESH
F32, BF16, I32 = jnp.float32, jnp.bfloat16, jnp.int32
NB = 48
HALF = NB // 2
QUARTER = HALF // 2
NO = 64
NY = 8
LANES = 128
FAR_FIRST = (4, 3, 5, 2, 6, 1, 7)
TILE_ORDER = (3, 5, 4, 1, 7, 2, 6, 0)


def remote(src, dst, send_sem, recv_sem, owner, dp):
    return pltpu.make_async_remote_copy(
        src_ref=src, dst_ref=dst, send_sem=send_sem, recv_sem=recv_sem,
        device_id={"owner": owner, "dp": dp}, device_id_type=MESH,
    )


def signal(sem, owner, dp):
    pl.semaphore_signal(sem, inc=1, device_id={"owner": owner, "dp": dp}, device_id_type=MESH)


def diagonal_column(row):
    sub = lax.broadcasted_iota(I32, (LANES, LANES), 0)
    lane = lax.broadcasted_iota(I32, (LANES, LANES), 1)
    return jnp.sum(jnp.where(sub == lane, row, 0), axis=1, keepdims=True)


def build_tables(map_ref, dims_ref, rows, table):
    rows[...] = jnp.full((8, LANES), -1, I32)
    rows[0:1, 0:NB] = map_ref[...]
    rows[1:3, 0:NB] = dims_ref[...]
    sub = lax.broadcasted_iota(I32, (LANES, LANES), 0)
    lane = lax.broadcasted_iota(I32, (LANES, LANES), 1)
    owner_row = rows[0:1, :]
    owner_col = diagonal_column(owner_row)
    live_rows = diagonal_column(rows[1:2, :])
    live_cols = diagonal_column(rows[2:3, :])
    same = owner_col == owner_row
    slot_row = jnp.sum(jnp.where(same & (sub < lane), 1, 0), axis=0, keepdims=True)
    slot_col = jnp.sum(jnp.where(same & (lane < sub), 1, 0), axis=1, keepdims=True)
    owned = owner_col == lane
    for slot in range(2):
        hit = owned & (slot_col == slot)
        for row, value in ((slot, sub), (2 + slot, live_rows), (4 + slot, live_cols)):
            table[row : row + 1, :] = jnp.sum(jnp.where(hit, value, 0), axis=0, keepdims=True)
    table[6:7, :] = owner_row
    table[7:8, :] = slot_row


def kernel(
    grads, map_ref, dims_ref, left, right, out_ref,
    g, gin, pair, far, mid, near, relayed, red, out1, in1, lv, rv, g32, prod, pin, dsc, xin, y32, out2, in2, f32s, rows, table, tab,
    load_sem, plane, core_s, core_r, rs_s, rs_r, red_s, red_r, a1_s, a1_r, e_s, e_r, x_s, x_r, a2_s, a2_r,
):
    me = lax.axis_index("owner")
    dp = lax.axis_index("dp")
    x, z = lax.div(me, 8), lax.rem(me, 8)
    y, c = lax.div(dp, 2), lax.rem(dp, 2)
    other = dp + 1 - 2 * c

    load_g = pltpu.make_async_copy(grads, g, load_sem.at[0])
    load_l = pltpu.make_async_copy(left.at[c], lv, load_sem.at[1])
    load_r = pltpu.make_async_copy(right.at[c], rv, load_sem.at[2])
    load_g.start()

    def along_x(i):
        return lax.rem(x + i, 8) * 8 + z

    def along_z(i):
        return x * 8 + lax.rem(z + i, 8)

    def owner_at(i):
        return lax.rem(x + lax.rem(i, 8), 8) * 8 + lax.rem(z + lax.div(i, 8), 8)

    def dp_at(offset):
        return lax.rem(y + offset, NY)

    pending = []
    barrier = pltpu.get_barrier_semaphore()
    signal(barrier, me, other)
    for offset in (1, 7, 2, 6):
        signal(barrier, me, dp_at(offset) * 2 + c)
    for i in range(1, 8):
        signal(barrier, along_x(i), dp)
        signal(barrier, along_z(i), dp)
    pl.semaphore_wait(barrier, 1 + 4 + 14)

    mine, theirs = c * HALF, (1 - c) * HALF
    load_g.wait()
    halves = {}
    for offset in TILE_ORDER:
        tile = pl.ds(pl.multiple_of(dp_at(offset) * LANES, LANES), LANES)
        copy = remote(
            g.at[pl.ds(theirs, HALF), :, tile], gin.at[offset], core_s.at[offset], core_r.at[offset], me, other
        )
        copy.start()
        pending.append(copy.wait_send)
        halves[offset] = (copy, tile)
    load_l.start()
    load_r.start()

    def core_sum(offset, b):
        return g[mine + b, :, halves[offset][1]].astype(F32) + gin[offset, b].astype(F32)

    def sum_blocks(offset, first, count, terms=()):
        def add(b, carry):
            acc = core_sum(offset, first + b)
            for buffer, way, start in terms:
                acc = acc + buffer[way, start + b].astype(F32)
            pair[offset, first + b] = acc.astype(BF16)
            return carry

        lax.fori_loop(0, count, add, 0, unroll=4)

    def send_sums(offset, first, count, target, buffer, k):
        copy = remote(
            pair.at[offset, pl.ds(first, count)], buffer, rs_s.at[k], rs_r.at[k], me, dp_at(target) * 2 + c
        )
        copy.start()
        pending.append(copy.wait_send)
        return copy

    ways = ((0, 2, 3, 1, 0, QUARTER), (1, 6, 5, 7, QUARTER, 0))
    arrivals = {}
    for way, own, three, step, both, alone in ways:
        halves[three][0].wait_recv()
        sum_blocks(three, alone, QUARTER)
        arrivals[way, "alone"] = send_sums(three, alone, QUARTER, step, mid.at[way, pl.ds(alone, QUARTER)], way)
    halves[4][0].wait_recv()
    for way, own, three, step, both, alone in ways:
        sum_blocks(4, both, QUARTER)
        arrivals[way, "far"] = send_sums(4, both, QUARTER, own, far.at[way], 2 + way)
    for way, own, three, step, both, alone in ways:
        sum_blocks(three, both, QUARTER)
        arrivals[way, "both"] = send_sums(three, both, QUARTER, step, mid.at[way, pl.ds(both, QUARTER)], 4 + way)
    for way, own, three, step, both, alone in ways:
        halves[step][0].wait_recv()
        sum_blocks(step, 0, HALF)
        arrivals[way, "near"] = send_sums(step, 0, HALF, step, near.at[way], 6 + way)
    for i in range(1, 8):
        signal(plane, along_x(i), dp)
    for way, own, three, step, both, alone in ways:
        halves[own][0].wait_recv()
        arrivals[way, "alone"].wait_recv()
        sum_blocks(own, alone, QUARTER, ((mid, way, alone),))
        arrivals[way, "first"] = send_sums(own, alone, QUARTER, own, relayed.at[way, pl.ds(alone, QUARTER)], 8 + way)
    for way, own, three, step, both, alone in ways:
        arrivals[way, "far"].wait_recv()
        arrivals[way, "both"].wait_recv()
        sum_blocks(own, both, QUARTER, ((mid, way, both), (far, way, 0)))
        arrivals[way, "last"] = send_sums(own, both, QUARTER, own, relayed.at[way, pl.ds(both, QUARTER)], 10 + way)

    build_tables(map_ref, dims_ref, rows, table)
    to_scalars = pltpu.make_async_copy(table, tab, load_sem.at[3])
    to_scalars.start()
    to_scalars.wait()

    halves[0][0].wait_recv()
    for way in range(2):
        for part in ("near", "first", "last"):
            arrivals[way, part].wait_recv()

    def total(b, carry):
        acc = core_sum(0, b)
        for way in range(2):
            acc = acc + near[way, b].astype(F32) + relayed[way, b].astype(F32)
        red[mine + b] = acc.astype(BF16)
        return carry

    lax.fori_loop(0, HALF, total, 0, unroll=4)
    share = remote(red.at[pl.ds(mine, HALF)], red.at[pl.ds(mine, HALF)], red_s, red_r, me, other)
    share.start()
    pending.append(share.wait_send)
    share.wait_recv()

    pl.semaphore_wait(plane, 7)

    def block_at(t):
        return jnp.clip(tab[c, t], 0, NB - 1)

    in1[me] = red[block_at(me)]

    def dispatch(i, carry):
        t = owner_at(i)
        out1[t] = red[block_at(t)]
        remote(out1.at[t], in1.at[me], a1_s, a1_r, t, dp).start()
        return carry

    lax.fori_loop(1, NO, dispatch, 0)
    pending.append(pltpu.make_async_copy(out1.at[pl.ds(0, NO - 1)], in1.at[pl.ds(0, NO - 1)], a1_s).wait)
    load_l.wait()
    pltpu.make_async_copy(out1.at[pl.ds(0, NO - 1)], in1.at[pl.ds(0, NO - 1)], a1_r).wait()

    live_rows, live_cols = tab[2 + c, me], tab[4 + c, me]
    in_columns = jnp.where(y < live_cols, 1, 0)
    row_limit = live_rows * 2 * in_columns

    def place(q, carry):
        tile = in1[q].astype(F32)
        keep = lax.broadcasted_iota(I32, (16, LANES), 0) < row_limit
        g32[pl.ds(q, 16, stride=NO), :] = jnp.where(keep, tile, 0.0)
        return carry

    lax.fori_loop(0, NO, place, 0, unroll=4)
    product = jnp.dot(lv[...], g32[pl.ds(0, 8 * LANES), :].astype(BF16), preferred_element_type=F32).astype(BF16)
    prod[...] = product.reshape(NY, LANES, LANES)

    my_tile = pl.ds(pl.multiple_of(y * LANES, LANES), LANES)
    bands = []
    for i, offset in enumerate(FAR_FIRST):
        t = dp_at(offset)
        copy = remote(prod.at[t], pin.at[:, my_tile], e_s.at[i], e_r.at[i], me, t * 2 + c)
        copy.start()
        pending.append(copy.wait_send)
        bands.append(copy)
    pin[:, my_tile] = prod[y]
    load_r.wait()
    for copy in bands:
        copy.wait_recv()
    update = jnp.dot(pin[...], rv[...], preferred_element_type=F32)
    column_limit = live_cols * LANES * jnp.where(y < live_rows, 1, 0)
    keep = lax.broadcasted_iota(I32, (LANES, 8 * LANES), 1) < column_limit
    update = jnp.where(keep, update, 0.0).astype(BF16)
    for half in range(2):
        for j in range(8):
            dsc[half, j] = update[half * NO : (half + 1) * NO, j * LANES : (j + 1) * LANES]
    swap = remote(dsc.at[1 - c], xin, x_s, x_r, me, other)
    swap.start()
    pending.append(swap.wait_send)
    for j in range(8):
        y32[pl.ds(c * 8 + j, NO, stride=16), :] = dsc[c, j].astype(F32)
    swap.wait_recv()
    for j in range(8):
        y32[pl.ds((1 - c) * 8 + j, NO, stride=16), :] = xin[j].astype(F32)
    out2[...] = y32[pl.ds(0, NO * 16), :].astype(BF16).reshape(NO, 16, LANES)

    in2[me] = out2[me]

    def give_back(i, carry):
        t = owner_at(i)
        remote(out2.at[t], in2.at[me], a2_s, a2_r, t, dp).start()
        return carry

    lax.fori_loop(1, NO, give_back, 0)
    pending.append(pltpu.make_async_copy(out2.at[pl.ds(0, NO - 1)], in2.at[pl.ds(0, NO - 1)], a2_s).wait)
    pltpu.make_async_copy(out2.at[pl.ds(0, NO - 1)], in2.at[pl.ds(0, NO - 1)], a2_r).wait()

    def pick(b, carry):
        both = in2[jnp.clip(tab[6, b], 0, NO - 1)].astype(F32)
        first = jnp.where(tab[7, b] == 0, 1, 0)
        chosen = jnp.where(first == 1, both[:8], both[8:])
        f32s[pl.ds(pl.multiple_of(b * 8, 8), 8), :] = chosen
        return carry

    lax.fori_loop(0, NB, pick, 0, unroll=4)
    for j in range(8):
        out_ref[:, j * LANES : (j + 1) * LANES] = f32s[pl.ds(j, NB, stride=8), :].astype(BF16)

    for wait in pending:
        wait()


def on_device(grads, owner_map, block_dims, left_root, right_root):
    any_spec = pl.BlockSpec(memory_space=pltpu.HBM)
    vmem_spec = pl.BlockSpec(memory_space=pltpu.VMEM)
    dma = pltpu.SemaphoreType.DMA
    out = pl.pallas_call(
        kernel,
        out_shape=jax.ShapeDtypeStruct((NB, 8 * LANES), BF16),
        in_specs=[any_spec, vmem_spec, vmem_spec, any_spec, any_spec],
        out_specs=vmem_spec,
        scratch_shapes=[
            pltpu.VMEM((NB, 16, 8 * LANES), BF16),
            pltpu.VMEM((8, HALF, 16, LANES), BF16),
            pltpu.VMEM((8, HALF, 16, LANES), BF16),
            pltpu.VMEM((2, QUARTER, 16, LANES), BF16),
            pltpu.VMEM((2, HALF, 16, LANES), BF16),
            pltpu.VMEM((2, HALF, 16, LANES), BF16),
            pltpu.VMEM((2, HALF, 16, LANES), BF16),
            pltpu.VMEM((NB, 16, LANES), BF16),
            pltpu.VMEM((NO, 16, LANES), BF16),
            pltpu.VMEM((NO, 16, LANES), BF16),
            pltpu.VMEM((8 * LANES, 8 * LANES), BF16),
            pltpu.VMEM((8 * LANES, 8 * LANES), BF16),
            pltpu.VMEM((8 * LANES + NO, LANES), F32),
            pltpu.VMEM((NY, LANES, LANES), BF16),
            pltpu.VMEM((LANES, 8 * LANES), BF16),
            pltpu.VMEM((2, 8, NO, LANES), BF16),
            pltpu.VMEM((8, NO, LANES), BF16),
            pltpu.VMEM((NO * 16 + 16, LANES), F32),
            pltpu.VMEM((NO, 16, LANES), BF16),
            pltpu.VMEM((NO, 16, LANES), BF16),
            pltpu.VMEM((NB * 8 + 8, LANES), F32),
            pltpu.VMEM((8, LANES), I32),
            pltpu.VMEM((8, LANES), I32),
            pltpu.SMEM((8, LANES), I32),
            dma((4,)),
            pltpu.SemaphoreType.REGULAR,
            dma((8,)), dma((8,)),
            dma((12,)), dma((12,)),
            dma, dma,
            dma, dma,
            dma((7,)), dma((7,)),
            dma, dma,
            dma, dma,
        ],
        compiler_params=pltpu.CompilerParams(
            collective_id=0, has_side_effects=True, vmem_limit_bytes=60 * 1024 * 1024
        ),
    )(
        grads.reshape(NB, 16, 8 * LANES),
        owner_map.reshape(1, NB),
        block_dims.T,
        left_root[0],
        right_root[0],
    )
    return out.reshape(NB, 1, 1, 8 * LANES)


def solution(mesh):
    placed = (
        P("dp", None, None, "owner", None),
        P(),
        P(),
        P("owner", None, None, None),
        P("owner", None, None, None),
    )
    return jax.shard_map(
        on_device,
        mesh=mesh,
        in_specs=placed,
        out_specs=P(None, "dp", "owner", None),
        check_vma=False,
    )
```

```python
import functools

import jax
import jax.numpy as jnp
from jax import lax
from jax.experimental import pallas as pl
from jax.experimental.pallas import tpu as pltpu
from jax.sharding import PartitionSpec as P

MESH = pl.DeviceIdType.MESH
F32, BF16, I32 = jnp.float32, jnp.bfloat16, jnp.int32
NB = 48
HALF = NB // 2
QUARTER = HALF // 2
NO = 64
NY = 8
LANES = 128
FAR_FIRST = (4, 3, 5, 2, 6, 1, 7)
TILE_ORDER = (3, 5, 4, 1, 7, 2, 6, 0)


def remote(src, dst, send_sem, recv_sem, owner, dp):
    return pltpu.make_async_remote_copy(
        src_ref=src, dst_ref=dst, send_sem=send_sem, recv_sem=recv_sem,
        device_id={"owner": owner, "dp": dp}, device_id_type=MESH,
    )


def signal(sem, owner, dp):
    pl.semaphore_signal(sem, inc=1, device_id={"owner": owner, "dp": dp}, device_id_type=MESH)


def diagonal_column(row):
    sub = lax.broadcasted_iota(I32, (LANES, LANES), 0)
    lane = lax.broadcasted_iota(I32, (LANES, LANES), 1)
    return jnp.sum(jnp.where(sub == lane, row, 0), axis=1, keepdims=True)


def build_tables(map_ref, dims_ref, rows, table):
    rows[...] = jnp.full((8, LANES), -1, I32)
    rows[0:1, 0:NB] = map_ref[...]
    rows[1:3, 0:NB] = dims_ref[...]
    sub = lax.broadcasted_iota(I32, (LANES, LANES), 0)
    lane = lax.broadcasted_iota(I32, (LANES, LANES), 1)
    owner_row = rows[0:1, :]
    owner_col = diagonal_column(owner_row)
    live_rows = diagonal_column(rows[1:2, :])
    live_cols = diagonal_column(rows[2:3, :])
    same = owner_col == owner_row
    slot_row = jnp.sum(jnp.where(same & (sub < lane), 1, 0), axis=0, keepdims=True)
    slot_col = jnp.sum(jnp.where(same & (lane < sub), 1, 0), axis=1, keepdims=True)
    owned = owner_col == lane
    for slot in range(2):
        hit = owned & (slot_col == slot)
        for row, value in ((slot, sub), (2 + slot, live_rows), (4 + slot, live_cols)):
            table[row : row + 1, :] = jnp.sum(jnp.where(hit, value, 0), axis=0, keepdims=True)
    table[6:7, :] = owner_row
    table[7:8, :] = slot_row


def kernel(
    grads, map_ref, dims_ref, left, right, out_ref,
    g, gin, pair, far, mid, near, relayed, red, out1, in1, lv, rv, g32, prod, pin, dsc, xin, y32, out2, in2, f32s, rows, table, tab,
    load_sem, plane, core_s, core_r, rs_s, rs_r, red_s, red_r, a1_s, a1_r, e_s, e_r, x_s, x_r, a2_s, a2_r,
):
    me = lax.axis_index("owner")
    dp = lax.axis_index("dp")
    x, z = lax.div(me, 8), lax.rem(me, 8)
    y, c = lax.div(dp, 2), lax.rem(dp, 2)
    other = dp + 1 - 2 * c

    load_g = pltpu.make_async_copy(grads, g, load_sem.at[0])
    load_l = pltpu.make_async_copy(left.at[c], lv, load_sem.at[1])
    load_r = pltpu.make_async_copy(right.at[c], rv, load_sem.at[2])
    load_g.start()

    def in_line(i):
        return lax.rem(x + i * c, 8) * 8 + lax.rem(z + i * (1 - c), 8)

    def owner_at(i):
        return lax.rem(x + lax.rem(i, 8), 8) * 8 + lax.rem(z + lax.div(i, 8), 8)

    def dp_at(offset):
        return lax.rem(y + offset, NY)

    pending = []
    barrier = pltpu.get_barrier_semaphore()
    signal(barrier, me, other)
    for offset in (1, 7, 2, 6):
        signal(barrier, me, dp_at(offset) * 2 + c)
    for i in range(1, 8):
        signal(barrier, in_line(i), dp)
    pl.semaphore_wait(barrier, 1 + 4 + 7)

    mine, theirs = c * HALF, (1 - c) * HALF
    load_g.wait()
    halves = {}
    for offset in TILE_ORDER:
        tile = pl.ds(pl.multiple_of(dp_at(offset) * LANES, LANES), LANES)
        copy = remote(
            g.at[pl.ds(theirs, HALF), :, tile], gin.at[offset], core_s.at[offset], core_r.at[offset], me, other
        )
        copy.start()
        pending.append(copy.wait_send)
        halves[offset] = (copy, tile)
    load_l.start()
    load_r.start()
    signal(plane.at[0], me, other)

    def core_sum(offset, b):
        return g[mine + b, :, halves[offset][1]].astype(F32) + gin[offset, b].astype(F32)

    def sum_blocks(offset, first, count, terms=()):
        def add(b, carry):
            acc = core_sum(offset, first + b)
            for buffer, way, start in terms:
                acc = acc + buffer[way, start + b].astype(F32)
            pair[offset, first + b] = acc.astype(BF16)
            return carry

        lax.fori_loop(0, count, add, 0, unroll=4)

    def send_sums(offset, first, count, target, buffer, k):
        copy = remote(
            pair.at[offset, pl.ds(first, count)], buffer, rs_s.at[k], rs_r.at[k], me, dp_at(target) * 2 + c
        )
        copy.start()
        pending.append(copy.wait_send)
        return copy

    ways = ((0, 2, 3, 1, 0, QUARTER), (1, 6, 5, 7, QUARTER, 0))
    arrivals = {}
    for way, own, three, step, both, alone in ways:
        halves[three][0].wait_recv()
        sum_blocks(three, alone, QUARTER)
        arrivals[way, "alone"] = send_sums(three, alone, QUARTER, step, mid.at[way, pl.ds(alone, QUARTER)], way)
    halves[4][0].wait_recv()
    for way, own, three, step, both, alone in ways:
        sum_blocks(4, both, QUARTER)
        arrivals[way, "far"] = send_sums(4, both, QUARTER, own, far.at[way], 2 + way)
    for way, own, three, step, both, alone in ways:
        sum_blocks(three, both, QUARTER)
        arrivals[way, "both"] = send_sums(three, both, QUARTER, step, mid.at[way, pl.ds(both, QUARTER)], 4 + way)
    for way, own, three, step, both, alone in ways:
        halves[step][0].wait_recv()
        sum_blocks(step, 0, HALF)
        arrivals[way, "near"] = send_sums(step, 0, HALF, step, near.at[way], 6 + way)
    pl.semaphore_wait(plane.at[0], 1)
    for i in range(1, 8):
        signal(plane.at[1], in_line(i), dp)
    for way, own, three, step, both, alone in ways:
        halves[own][0].wait_recv()
        arrivals[way, "alone"].wait_recv()
        sum_blocks(own, alone, QUARTER, ((mid, way, alone),))
        arrivals[way, "first"] = send_sums(own, alone, QUARTER, own, relayed.at[way, pl.ds(alone, QUARTER)], 8 + way)
    for way, own, three, step, both, alone in ways:
        arrivals[way, "far"].wait_recv()
        arrivals[way, "both"].wait_recv()
        sum_blocks(own, both, QUARTER, ((mid, way, both), (far, way, 0)))
        arrivals[way, "last"] = send_sums(own, both, QUARTER, own, relayed.at[way, pl.ds(both, QUARTER)], 10 + way)

    pl.semaphore_wait(plane.at[1], 7)
    signal(plane.at[2], me, other)
    build_tables(map_ref, dims_ref, rows, table)
    to_scalars = pltpu.make_async_copy(table, tab, load_sem.at[3])
    to_scalars.start()
    to_scalars.wait()

    halves[0][0].wait_recv()
    for way in range(2):
        for part in ("near", "first", "last"):
            arrivals[way, part].wait_recv()

    def total(b, carry):
        acc = core_sum(0, b)
        for way in range(2):
            acc = acc + near[way, b].astype(F32) + relayed[way, b].astype(F32)
        red[mine + b] = acc.astype(BF16)
        return carry

    lax.fori_loop(0, HALF, total, 0, unroll=4)
    share = remote(red.at[pl.ds(mine, HALF)], red.at[pl.ds(mine, HALF)], red_s, red_r, me, other)
    share.start()
    pending.append(share.wait_send)
    share.wait_recv()

    pl.semaphore_wait(plane.at[2], 1)

    def block_at(t):
        return jnp.clip(tab[c, t], 0, NB - 1)

    in1[me] = red[block_at(me)]

    def dispatch(i, carry):
        t = owner_at(i)
        out1[t] = red[block_at(t)]
        remote(out1.at[t], in1.at[me], a1_s, a1_r, t, dp).start()
        return carry

    lax.fori_loop(1, NO, dispatch, 0)
    pending.append(pltpu.make_async_copy(out1.at[pl.ds(0, NO - 1)], in1.at[pl.ds(0, NO - 1)], a1_s).wait)
    load_l.wait()
    pltpu.make_async_copy(out1.at[pl.ds(0, NO - 1)], in1.at[pl.ds(0, NO - 1)], a1_r).wait()

    live_rows, live_cols = tab[2 + c, me], tab[4 + c, me]
    in_columns = jnp.where(y < live_cols, 1, 0)
    row_limit = live_rows * 2 * in_columns

    def place(q, carry):
        tile = in1[q].astype(F32)
        keep = lax.broadcasted_iota(I32, (16, LANES), 0) < row_limit
        g32[pl.ds(q, 16, stride=NO), :] = jnp.where(keep, tile, 0.0)
        return carry

    lax.fori_loop(0, NO, place, 0, unroll=4)
    masked = g32[pl.ds(0, 8 * LANES), :].astype(BF16)

    my_tile = pl.ds(pl.multiple_of(y * LANES, LANES), LANES)

    def band(t):
        rows_of_band = lv[pl.ds(pl.multiple_of(t * LANES, LANES), LANES), :]
        return jnp.dot(rows_of_band, masked, preferred_element_type=F32).astype(BF16)

    bands = []
    for i, offset in enumerate(FAR_FIRST):
        t = dp_at(offset)
        prod[i] = band(t)
        copy = remote(prod.at[i], pin.at[:, my_tile], e_s.at[i], e_r.at[i], me, t * 2 + c)
        copy.start()
        pending.append(copy.wait_send)
        bands.append(copy)
    pin[:, my_tile] = band(y)
    load_r.wait()
    for copy in bands:
        copy.wait_recv()
    column_limit = live_cols * LANES * jnp.where(y < live_rows, 1, 0)
    keep = lax.broadcasted_iota(I32, (NO, 8 * LANES), 1) < column_limit

    def update(half):
        rows_of_half = pin[pl.ds(pl.multiple_of(half * NO, NO), NO), :]
        return jnp.where(keep, jnp.dot(rows_of_half, rv[...], preferred_element_type=F32), 0.0)

    given = update(1 - c).astype(BF16)
    for j in range(8):
        dsc[j] = given[:, j * LANES : (j + 1) * LANES]
    swap = remote(dsc, xin, x_s, x_r, me, other)
    swap.start()
    pending.append(swap.wait_send)
    kept = update(c)
    for j in range(8):
        y32[pl.ds(c * 8 + j, NO, stride=16), :] = kept[:, j * LANES : (j + 1) * LANES]
    swap.wait_recv()
    for j in range(8):
        y32[pl.ds((1 - c) * 8 + j, NO, stride=16), :] = xin[j].astype(F32)
    out2[...] = y32[pl.ds(0, NO * 16), :].astype(BF16).reshape(NO, 16, LANES)

    in2[me] = out2[me]

    def give_back(i, carry):
        t = owner_at(i)
        remote(out2.at[t], in2.at[me], a2_s, a2_r, t, dp).start()
        return carry

    lax.fori_loop(1, NO, give_back, 0)
    pending.append(pltpu.make_async_copy(out2.at[pl.ds(0, NO - 1)], in2.at[pl.ds(0, NO - 1)], a2_s).wait)
    pltpu.make_async_copy(out2.at[pl.ds(0, NO - 1)], in2.at[pl.ds(0, NO - 1)], a2_r).wait()

    def pick(b, carry):
        both = in2[jnp.clip(tab[6, b], 0, NO - 1)].astype(F32)
        first = jnp.where(tab[7, b] == 0, 1, 0)
        chosen = jnp.where(first == 1, both[:8], both[8:])
        f32s[pl.ds(pl.multiple_of(b * 8, 8), 8), :] = chosen
        return carry

    lax.fori_loop(0, NB, pick, 0, unroll=8)
    for j in range(8):
        out_ref[:, j * LANES : (j + 1) * LANES] = f32s[pl.ds(j, NB, stride=8), :].astype(BF16)

    for wait in pending:
        wait()


def on_device(grads, owner_map, block_dims, left_root, right_root):
    any_spec = pl.BlockSpec(memory_space=pltpu.HBM)
    vmem_spec = pl.BlockSpec(memory_space=pltpu.VMEM)
    dma = pltpu.SemaphoreType.DMA
    out = pl.pallas_call(
        kernel,
        out_shape=jax.ShapeDtypeStruct((NB, 8 * LANES), BF16),
        in_specs=[any_spec, vmem_spec, vmem_spec, any_spec, any_spec],
        out_specs=vmem_spec,
        scratch_shapes=[
            pltpu.VMEM((NB, 16, 8 * LANES), BF16),
            pltpu.VMEM((8, HALF, 16, LANES), BF16),
            pltpu.VMEM((8, HALF, 16, LANES), BF16),
            pltpu.VMEM((2, QUARTER, 16, LANES), BF16),
            pltpu.VMEM((2, HALF, 16, LANES), BF16),
            pltpu.VMEM((2, HALF, 16, LANES), BF16),
            pltpu.VMEM((2, HALF, 16, LANES), BF16),
            pltpu.VMEM((NB, 16, LANES), BF16),
            pltpu.VMEM((NO, 16, LANES), BF16),
            pltpu.VMEM((NO, 16, LANES), BF16),
            pltpu.VMEM((8 * LANES, 8 * LANES), BF16),
            pltpu.VMEM((8 * LANES, 8 * LANES), BF16),
            pltpu.VMEM((8 * LANES + NO, LANES), F32),
            pltpu.VMEM((NY - 1, LANES, LANES), BF16),
            pltpu.VMEM((LANES, 8 * LANES), BF16),
            pltpu.VMEM((8, NO, LANES), BF16),
            pltpu.VMEM((8, NO, LANES), BF16),
            pltpu.VMEM((NO * 16 + 16, LANES), F32),
            pltpu.VMEM((NO, 16, LANES), BF16),
            pltpu.VMEM((NO, 16, LANES), BF16),
            pltpu.VMEM((NB * 8 + 8, LANES), F32),
            pltpu.VMEM((8, LANES), I32),
            pltpu.VMEM((8, LANES), I32),
            pltpu.SMEM((8, LANES), I32),
            dma((4,)),
            pltpu.SemaphoreType.REGULAR((3,)),
            dma((8,)), dma((8,)),
            dma((12,)), dma((12,)),
            dma, dma,
            dma, dma,
            dma((7,)), dma((7,)),
            dma, dma,
            dma, dma,
        ],
        compiler_params=pltpu.CompilerParams(
            collective_id=0, has_side_effects=True, vmem_limit_bytes=60 * 1024 * 1024
        ),
    )(
        grads.reshape(NB, 16, 8 * LANES),
        owner_map.reshape(1, NB),
        block_dims.T,
        left_root[0],
        right_root[0],
    )
    return out.reshape(NB, 1, 1, 8 * LANES)


def solution(mesh):
    placed = (
        P("dp", None, None, "owner", None),
        P(),
        P(),
        P("owner", None, None, None),
        P("owner", None, None, None),
    )
    return jax.shard_map(
        on_device,
        mesh=mesh,
        in_specs=placed,
        out_specs=P(None, "dp", "owner", None),
        check_vma=False,
    )
```

```python
import functools

import jax
import jax.numpy as jnp
from jax import lax
from jax.experimental import pallas as pl
from jax.experimental.pallas import tpu as pltpu
from jax.sharding import PartitionSpec as P

MESH = pl.DeviceIdType.MESH
F32, BF16, I32 = jnp.float32, jnp.bfloat16, jnp.int32
NB = 48
HALF = NB // 2
QUARTER = HALF // 2
NO = 64
NY = 8
LANES = 128
FAR_FIRST = (4, 3, 5, 2, 6, 1, 7)
TILE_ORDER = (3, 5, 4, 1, 7, 2, 6, 0)


def remote(src, dst, send_sem, recv_sem, owner, dp):
    return pltpu.make_async_remote_copy(
        src_ref=src, dst_ref=dst, send_sem=send_sem, recv_sem=recv_sem,
        device_id={"owner": owner, "dp": dp}, device_id_type=MESH,
    )


def signal(sem, owner, dp):
    pl.semaphore_signal(sem, inc=1, device_id={"owner": owner, "dp": dp}, device_id_type=MESH)


def diagonal_column(row):
    sub = lax.broadcasted_iota(I32, (LANES, LANES), 0)
    lane = lax.broadcasted_iota(I32, (LANES, LANES), 1)
    return jnp.sum(jnp.where(sub == lane, row, 0), axis=1, keepdims=True)


def build_tables(map_ref, dims_ref, rows, table):
    rows[...] = jnp.full((8, LANES), -1, I32)
    rows[0:1, 0:NB] = map_ref[...]
    rows[1:3, 0:NB] = dims_ref[...]
    sub = lax.broadcasted_iota(I32, (LANES, LANES), 0)
    lane = lax.broadcasted_iota(I32, (LANES, LANES), 1)
    owner_row = rows[0:1, :]
    owner_col = diagonal_column(owner_row)
    live_rows = diagonal_column(rows[1:2, :])
    live_cols = diagonal_column(rows[2:3, :])
    same = owner_col == owner_row
    slot_row = jnp.sum(jnp.where(same & (sub < lane), 1, 0), axis=0, keepdims=True)
    slot_col = jnp.sum(jnp.where(same & (lane < sub), 1, 0), axis=1, keepdims=True)
    owned = owner_col == lane
    for slot in range(2):
        hit = owned & (slot_col == slot)
        for row, value in ((slot, sub), (2 + slot, live_rows), (4 + slot, live_cols)):
            table[row : row + 1, :] = jnp.sum(jnp.where(hit, value, 0), axis=0, keepdims=True)
    table[6:7, :] = owner_row
    table[7:8, :] = slot_row


def kernel(
    grads, map_ref, dims_ref, left, right, out_ref,
    g, gin, pair, far, mid, near, relayed, red, out1, in1, lv, rv, g32, prod, pin, dsc, xin, y32, out2, in2, f32s, rows, table, tab,
    load_sem, plane, core_s, core_r, rs_s, rs_r, red_s, red_r, a1_s, a1_r, e_s, e_r, x_s, x_r, a2_s, a2_r,
):
    me = lax.axis_index("owner")
    dp = lax.axis_index("dp")
    x, z = lax.div(me, 8), lax.rem(me, 8)
    y, c = lax.div(dp, 2), lax.rem(dp, 2)
    other = dp + 1 - 2 * c

    load_g = pltpu.make_async_copy(grads, g, load_sem.at[0])
    load_l = pltpu.make_async_copy(left.at[c], lv, load_sem.at[1])
    load_r = pltpu.make_async_copy(right.at[c], rv, load_sem.at[2])
    load_g.start()

    def in_line(i):
        return lax.rem(x + i * c, 8) * 8 + lax.rem(z + i * (1 - c), 8)

    def far_first(i):
        return 4 + lax.div(i + 1, 2) * (1 - 2 * lax.rem(i, 2))

    def owner_at(i):
        return lax.rem(x + far_first(lax.rem(i, 8)), 8) * 8 + lax.rem(z + far_first(lax.div(i, 8)), 8)

    def dp_at(offset):
        return lax.rem(y + offset, NY)

    pending = []
    barrier = pltpu.get_barrier_semaphore()
    signal(barrier, me, other)
    for offset in (1, 7, 2, 6):
        signal(barrier, me, dp_at(offset) * 2 + c)
    for i in range(1, 8):
        signal(barrier, in_line(i), dp)
    pl.semaphore_wait(barrier, 1 + 4 + 7)

    mine, theirs = c * HALF, (1 - c) * HALF
    load_g.wait()
    halves = {}
    for offset in TILE_ORDER:
        tile = pl.ds(pl.multiple_of(dp_at(offset) * LANES, LANES), LANES)
        copy = remote(
            g.at[pl.ds(theirs, HALF), :, tile], gin.at[offset], core_s.at[offset], core_r.at[offset], me, other
        )
        copy.start()
        pending.append(copy.wait_send)
        halves[offset] = (copy, tile)
    load_l.start()
    load_r.start()
    signal(plane.at[0], me, other)

    def core_sum(offset, b):
        return g[mine + b, :, halves[offset][1]].astype(F32) + gin[offset, b].astype(F32)

    def sum_blocks(offset, first, count, terms=()):
        def add(b, carry):
            acc = core_sum(offset, first + b)
            for buffer, way, start in terms:
                acc = acc + buffer[way, start + b].astype(F32)
            pair[offset, first + b] = acc.astype(BF16)
            return carry

        lax.fori_loop(0, count, add, 0, unroll=4)

    def send_sums(offset, first, count, target, buffer, k):
        copy = remote(
            pair.at[offset, pl.ds(first, count)], buffer, rs_s.at[k], rs_r.at[k], me, dp_at(target) * 2 + c
        )
        copy.start()
        pending.append(copy.wait_send)
        return copy

    ways = ((0, 2, 3, 1, 0, QUARTER), (1, 6, 5, 7, QUARTER, 0))
    arrivals = {}
    for way, own, three, step, both, alone in ways:
        halves[three][0].wait_recv()
        sum_blocks(three, alone, QUARTER)
        arrivals[way, "alone"] = send_sums(three, alone, QUARTER, step, mid.at[way, pl.ds(alone, QUARTER)], way)
    halves[4][0].wait_recv()
    for way, own, three, step, both, alone in ways:
        sum_blocks(4, both, QUARTER)
        arrivals[way, "far"] = send_sums(4, both, QUARTER, own, far.at[way], 2 + way)
    for way, own, three, step, both, alone in ways:
        sum_blocks(three, both, QUARTER)
        arrivals[way, "both"] = send_sums(three, both, QUARTER, step, mid.at[way, pl.ds(both, QUARTER)], 4 + way)
    for way, own, three, step, both, alone in ways:
        halves[step][0].wait_recv()
        sum_blocks(step, 0, HALF)
        arrivals[way, "near"] = send_sums(step, 0, HALF, step, near.at[way], 6 + way)
    pl.semaphore_wait(plane.at[0], 1)
    for i in range(1, 8):
        signal(plane.at[1], in_line(i), dp)
    for way, own, three, step, both, alone in ways:
        halves[own][0].wait_recv()
        arrivals[way, "alone"].wait_recv()
        sum_blocks(own, alone, QUARTER, ((mid, way, alone),))
        arrivals[way, "first"] = send_sums(own, alone, QUARTER, own, relayed.at[way, pl.ds(alone, QUARTER)], 8 + way)
    for way, own, three, step, both, alone in ways:
        arrivals[way, "far"].wait_recv()
        arrivals[way, "both"].wait_recv()
        sum_blocks(own, both, QUARTER, ((mid, way, both), (far, way, 0)))
        arrivals[way, "last"] = send_sums(own, both, QUARTER, own, relayed.at[way, pl.ds(both, QUARTER)], 10 + way)

    pl.semaphore_wait(plane.at[1], 7)
    signal(plane.at[2], me, other)
    build_tables(map_ref, dims_ref, rows, table)
    to_scalars = pltpu.make_async_copy(table, tab, load_sem.at[3])
    to_scalars.start()
    to_scalars.wait()

    halves[0][0].wait_recv()
    for way in range(2):
        for part in ("near", "first", "last"):
            arrivals[way, part].wait_recv()

    def total(b, carry):
        acc = core_sum(0, b)
        for way in range(2):
            acc = acc + near[way, b].astype(F32) + relayed[way, b].astype(F32)
        red[mine + b] = acc.astype(BF16)
        return carry

    lax.fori_loop(0, HALF, total, 0, unroll=4)
    share = remote(red.at[pl.ds(mine, HALF)], red.at[pl.ds(mine, HALF)], red_s, red_r, me, other)
    share.start()
    pending.append(share.wait_send)
    share.wait_recv()

    pl.semaphore_wait(plane.at[2], 1)

    def block_at(t):
        return jnp.clip(tab[c, t], 0, NB - 1)

    in1[me] = red[block_at(me)]

    def dispatch(i, carry):
        t = owner_at(i)
        out1[t] = red[block_at(t)]
        remote(out1.at[t], in1.at[me], a1_s, a1_r, t, dp).start()
        return carry

    lax.fori_loop(0, NO - 1, dispatch, 0)
    pending.append(pltpu.make_async_copy(out1.at[pl.ds(0, NO - 1)], in1.at[pl.ds(0, NO - 1)], a1_s).wait)
    load_l.wait()
    pltpu.make_async_copy(out1.at[pl.ds(0, NO - 1)], in1.at[pl.ds(0, NO - 1)], a1_r).wait()

    live_rows, live_cols = tab[2 + c, me], tab[4 + c, me]
    in_columns = jnp.where(y < live_cols, 1, 0)
    row_limit = live_rows * 2 * in_columns

    def place(q, carry):
        tile = in1[q].astype(F32)
        keep = lax.broadcasted_iota(I32, (16, LANES), 0) < row_limit
        g32[pl.ds(q, 16, stride=NO), :] = jnp.where(keep, tile, 0.0)
        return carry

    lax.fori_loop(0, NO, place, 0, unroll=4)
    masked = g32[pl.ds(0, 8 * LANES), :].astype(BF16)

    my_tile = pl.ds(pl.multiple_of(y * LANES, LANES), LANES)

    def half_band(t, half):
        rows_of_band = lv[pl.ds(pl.multiple_of(t * LANES + half * NO, NO), NO), :]
        return jnp.dot(rows_of_band, masked, preferred_element_type=F32).astype(BF16)

    def send_half(part, half):
        at = pl.ds(pl.multiple_of(half * NO, NO), NO)
        copies = []
        for i, offset in enumerate(FAR_FIRST):
            t = dp_at(offset)
            prod[part, i] = half_band(t, half)
            copy = remote(
                prod.at[part, i], pin.at[at, my_tile], e_s.at[part, i], e_r.at[part, i], me, t * 2 + c
            )
            copy.start()
            pending.append(copy.wait_send)
            copies.append(copy)
        pin[at, my_tile] = half_band(y, half)
        return copies

    theirs_first = send_half(0, 1 - c)
    mine_next = send_half(1, c)
    load_r.wait()
    for copy in theirs_first:
        copy.wait_recv()
    column_limit = live_cols * LANES * jnp.where(y < live_rows, 1, 0)
    keep = lax.broadcasted_iota(I32, (NO, 8 * LANES), 1) < column_limit

    def update(half):
        rows_of_half = pin[pl.ds(pl.multiple_of(half * NO, NO), NO), :]
        return jnp.where(keep, jnp.dot(rows_of_half, rv[...], preferred_element_type=F32), 0.0)

    given = update(1 - c).astype(BF16)
    for j in range(8):
        dsc[j] = given[:, j * LANES : (j + 1) * LANES]
    swap = remote(dsc, xin, x_s, x_r, me, other)
    swap.start()
    pending.append(swap.wait_send)
    for copy in mine_next:
        copy.wait_recv()
    kept = update(c)
    for j in range(8):
        y32[pl.ds(c * 8 + j, NO, stride=16), :] = kept[:, j * LANES : (j + 1) * LANES]
    swap.wait_recv()
    for j in range(8):
        y32[pl.ds((1 - c) * 8 + j, NO, stride=16), :] = xin[j].astype(F32)
    out2[...] = y32[pl.ds(0, NO * 16), :].astype(BF16).reshape(NO, 16, LANES)

    in2[me] = out2[me]

    def give_back(i, carry):
        t = owner_at(i)
        remote(out2.at[t], in2.at[me], a2_s, a2_r, t, dp).start()
        return carry

    lax.fori_loop(0, NO - 1, give_back, 0)
    pending.append(pltpu.make_async_copy(out2.at[pl.ds(0, NO - 1)], in2.at[pl.ds(0, NO - 1)], a2_s).wait)
    pltpu.make_async_copy(out2.at[pl.ds(0, NO - 1)], in2.at[pl.ds(0, NO - 1)], a2_r).wait()

    def pick(b, carry):
        both = in2[jnp.clip(tab[6, b], 0, NO - 1)].astype(F32)
        first = jnp.where(tab[7, b] == 0, 1, 0)
        chosen = jnp.where(first == 1, both[:8], both[8:])
        f32s[pl.ds(pl.multiple_of(b * 8, 8), 8), :] = chosen
        return carry

    lax.fori_loop(0, NB, pick, 0, unroll=8)
    for j in range(8):
        out_ref[:, j * LANES : (j + 1) * LANES] = f32s[pl.ds(j, NB, stride=8), :].astype(BF16)

    for wait in pending:
        wait()


def on_device(grads, owner_map, block_dims, left_root, right_root):
    any_spec = pl.BlockSpec(memory_space=pltpu.HBM)
    vmem_spec = pl.BlockSpec(memory_space=pltpu.VMEM)
    dma = pltpu.SemaphoreType.DMA
    out = pl.pallas_call(
        kernel,
        out_shape=jax.ShapeDtypeStruct((NB, 8 * LANES), BF16),
        in_specs=[any_spec, vmem_spec, vmem_spec, any_spec, any_spec],
        out_specs=vmem_spec,
        scratch_shapes=[
            pltpu.VMEM((NB, 16, 8 * LANES), BF16),
            pltpu.VMEM((8, HALF, 16, LANES), BF16),
            pltpu.VMEM((8, HALF, 16, LANES), BF16),
            pltpu.VMEM((2, QUARTER, 16, LANES), BF16),
            pltpu.VMEM((2, HALF, 16, LANES), BF16),
            pltpu.VMEM((2, HALF, 16, LANES), BF16),
            pltpu.VMEM((2, HALF, 16, LANES), BF16),
            pltpu.VMEM((NB, 16, LANES), BF16),
            pltpu.VMEM((NO, 16, LANES), BF16),
            pltpu.VMEM((NO, 16, LANES), BF16),
            pltpu.VMEM((8 * LANES, 8 * LANES), BF16),
            pltpu.VMEM((8 * LANES, 8 * LANES), BF16),
            pltpu.VMEM((8 * LANES + NO, LANES), F32),
            pltpu.VMEM((2, NY - 1, NO, LANES), BF16),
            pltpu.VMEM((LANES, 8 * LANES), BF16),
            pltpu.VMEM((8, NO, LANES), BF16),
            pltpu.VMEM((8, NO, LANES), BF16),
            pltpu.VMEM((NO * 16 + 16, LANES), F32),
            pltpu.VMEM((NO, 16, LANES), BF16),
            pltpu.VMEM((NO, 16, LANES), BF16),
            pltpu.VMEM((NB * 8 + 8, LANES), F32),
            pltpu.VMEM((8, LANES), I32),
            pltpu.VMEM((8, LANES), I32),
            pltpu.SMEM((8, LANES), I32),
            dma((4,)),
            pltpu.SemaphoreType.REGULAR((3,)),
            dma((8,)), dma((8,)),
            dma((12,)), dma((12,)),
            dma, dma,
            dma, dma,
            dma((2, 7)), dma((2, 7)),
            dma, dma,
            dma, dma,
        ],
        compiler_params=pltpu.CompilerParams(
            collective_id=0, has_side_effects=True, vmem_limit_bytes=60 * 1024 * 1024
        ),
    )(
        grads.reshape(NB, 16, 8 * LANES),
        owner_map.reshape(1, NB),
        block_dims.T,
        left_root[0],
        right_root[0],
    )
    return out.reshape(NB, 1, 1, 8 * LANES)


def solution(mesh):
    placed = (
        P("dp", None, None, "owner", None),
        P(),
        P(),
        P("owner", None, None, None),
        P("owner", None, None, None),
    )
    return jax.shard_map(
        on_device,
        mesh=mesh,
        in_specs=placed,
        out_specs=P(None, "dp", "owner", None),
        check_vma=False,
    )
```

```python
import functools

import jax
import jax.numpy as jnp
from jax import lax
from jax.experimental import pallas as pl
from jax.experimental.pallas import tpu as pltpu
from jax.sharding import PartitionSpec as P

MESH = pl.DeviceIdType.MESH
F32, BF16, I32 = jnp.float32, jnp.bfloat16, jnp.int32
NB = 48
HALF = NB // 2
QUARTER = HALF // 2
NO = 64
NY = 8
LANES = 128
FAR_FIRST = (4, 3, 5, 2, 6, 1, 7)
TILE_ORDER = (3, 5, 4, 1, 7, 2, 6, 0)


def remote(src, dst, send_sem, recv_sem, owner, dp):
    return pltpu.make_async_remote_copy(
        src_ref=src, dst_ref=dst, send_sem=send_sem, recv_sem=recv_sem,
        device_id={"owner": owner, "dp": dp}, device_id_type=MESH,
    )


def signal(sem, owner, dp):
    pl.semaphore_signal(sem, inc=1, device_id={"owner": owner, "dp": dp}, device_id_type=MESH)


def diagonal_column(row):
    sub = lax.broadcasted_iota(I32, (LANES, LANES), 0)
    lane = lax.broadcasted_iota(I32, (LANES, LANES), 1)
    return jnp.sum(jnp.where(sub == lane, row, 0), axis=1, keepdims=True)


def build_tables(map_ref, dims_ref, rows, table):
    rows[...] = jnp.full((8, LANES), -1, I32)
    rows[0:1, 0:NB] = map_ref[...]
    rows[1:3, 0:NB] = dims_ref[...]
    sub = lax.broadcasted_iota(I32, (LANES, LANES), 0)
    lane = lax.broadcasted_iota(I32, (LANES, LANES), 1)
    owner_row = rows[0:1, :]
    owner_col = diagonal_column(owner_row)
    live_rows = diagonal_column(rows[1:2, :])
    live_cols = diagonal_column(rows[2:3, :])
    same = owner_col == owner_row
    slot_row = jnp.sum(jnp.where(same & (sub < lane), 1, 0), axis=0, keepdims=True)
    slot_col = jnp.sum(jnp.where(same & (lane < sub), 1, 0), axis=1, keepdims=True)
    owned = owner_col == lane
    for slot in range(2):
        hit = owned & (slot_col == slot)
        for row, value in ((slot, sub), (2 + slot, live_rows), (4 + slot, live_cols)):
            table[row : row + 1, :] = jnp.sum(jnp.where(hit, value, 0), axis=0, keepdims=True)
    table[6:7, :] = owner_row
    table[7:8, :] = slot_row


def kernel(
    grads, map_ref, dims_ref, left, right, out_ref,
    g, gin, pair, far, mid, near, relayed, red, out1, in1, lv, rv, g32, prod, pin, dsc, xin, y32, out2, in2, f32s, rows, table, tab,
    load_sem, plane, core_s, core_r, rs_s, rs_r, red_s, red_r, a1_s, a1_r, e_s, e_r, x_s, x_r, a2_s, a2_r,
):
    me = lax.axis_index("owner")
    dp = lax.axis_index("dp")
    x, z = lax.div(me, 8), lax.rem(me, 8)
    y, c = lax.div(dp, 2), lax.rem(dp, 2)
    other = dp + 1 - 2 * c

    load_g = pltpu.make_async_copy(grads.at[pl.ds(c * HALF, HALF)], g, load_sem.at[0])
    load_l = pltpu.make_async_copy(left.at[c], lv, load_sem.at[1])
    load_r = pltpu.make_async_copy(right.at[c], rv, load_sem.at[2])
    load_g.start()

    def in_line(i):
        return lax.rem(x + i * c, 8) * 8 + lax.rem(z + i * (1 - c), 8)

    def far_first(i):
        return 4 + lax.div(i + 1, 2) * (1 - 2 * lax.rem(i, 2))

    def owner_at(i):
        return lax.rem(x + far_first(lax.rem(i, 8)), 8) * 8 + lax.rem(z + far_first(lax.div(i, 8)), 8)

    def dp_at(offset):
        return lax.rem(y + offset, NY)

    pending = []
    barrier = pltpu.get_barrier_semaphore()
    signal(barrier, me, other)
    for offset in (1, 7, 2, 6):
        signal(barrier, me, dp_at(offset) * 2 + c)
    for i in range(1, 8):
        signal(barrier, in_line(i), dp)
    pl.semaphore_wait(barrier, 1 + 4 + 7)

    mine, theirs = c * HALF, (1 - c) * HALF
    halves = {}
    for offset in TILE_ORDER:
        tile = pl.ds(pl.multiple_of(dp_at(offset) * LANES, LANES), LANES)
        copy = remote(
            grads.at[pl.ds(theirs, HALF), :, tile], gin.at[offset], core_s.at[offset], core_r.at[offset], me, other
        )
        copy.start()
        pending.append(copy.wait_send)
        halves[offset] = (copy, tile)
    load_l.start()
    load_r.start()
    signal(plane.at[0], me, other)

    def core_sum(offset, b):
        return g[b, :, halves[offset][1]].astype(F32) + gin[offset, b].astype(F32)

    def sum_blocks(offset, first, count, terms=()):
        def add(b, carry):
            acc = core_sum(offset, first + b)
            for buffer, way, start in terms:
                acc = acc + buffer[way, start + b].astype(F32)
            pair[offset, first + b] = acc.astype(BF16)
            return carry

        lax.fori_loop(0, count, add, 0, unroll=4)

    def send_sums(offset, first, count, target, buffer, k):
        copy = remote(
            pair.at[offset, pl.ds(first, count)], buffer, rs_s.at[k], rs_r.at[k], me, dp_at(target) * 2 + c
        )
        copy.start()
        pending.append(copy.wait_send)
        return copy

    ways = ((0, 2, 3, 1, 0, QUARTER), (1, 6, 5, 7, QUARTER, 0))
    arrivals = {}
    load_g.wait()
    for way, own, three, step, both, alone in ways:
        halves[three][0].wait_recv()
        sum_blocks(three, alone, QUARTER)
        arrivals[way, "alone"] = send_sums(three, alone, QUARTER, step, mid.at[way, pl.ds(alone, QUARTER)], way)
    halves[4][0].wait_recv()
    for way, own, three, step, both, alone in ways:
        sum_blocks(4, both, QUARTER)
        arrivals[way, "far"] = send_sums(4, both, QUARTER, own, far.at[way], 2 + way)
    for way, own, three, step, both, alone in ways:
        sum_blocks(three, both, QUARTER)
        arrivals[way, "both"] = send_sums(three, both, QUARTER, step, mid.at[way, pl.ds(both, QUARTER)], 4 + way)
    for way, own, three, step, both, alone in ways:
        halves[step][0].wait_recv()
        sum_blocks(step, 0, HALF)
        arrivals[way, "near"] = send_sums(step, 0, HALF, step, near.at[way], 6 + way)
    pl.semaphore_wait(plane.at[0], 1)
    for i in range(1, 8):
        signal(plane.at[1], in_line(i), dp)
    for way, own, three, step, both, alone in ways:
        halves[own][0].wait_recv()
        arrivals[way, "alone"].wait_recv()
        sum_blocks(own, alone, QUARTER, ((mid, way, alone),))
        arrivals[way, "first"] = send_sums(own, alone, QUARTER, own, relayed.at[way, pl.ds(alone, QUARTER)], 8 + way)
    for way, own, three, step, both, alone in ways:
        arrivals[way, "far"].wait_recv()
        arrivals[way, "both"].wait_recv()
        sum_blocks(own, both, QUARTER, ((mid, way, both), (far, way, 0)))
        arrivals[way, "last"] = send_sums(own, both, QUARTER, own, relayed.at[way, pl.ds(both, QUARTER)], 10 + way)

    pl.semaphore_wait(plane.at[1], 7)
    signal(plane.at[2], me, other)
    build_tables(map_ref, dims_ref, rows, table)
    to_scalars = pltpu.make_async_copy(table, tab, load_sem.at[3])
    to_scalars.start()
    to_scalars.wait()

    load_l.wait()
    new_row = lax.broadcasted_iota(I32, (LANES, LANES), 0)
    old_row = (new_row // 32) % 2 * NO + new_row % 32 * 2 + new_row // NO
    reorder = jnp.where(lax.broadcasted_iota(I32, (LANES, LANES), 1) == old_row, 1.0, 0.0).astype(BF16)

    def reorder_band(t, carry):
        at = pl.ds(pl.multiple_of(t * LANES, LANES), LANES)
        lv[at, :] = jnp.dot(reorder, lv[at, :], preferred_element_type=F32).astype(BF16)
        return carry

    lax.fori_loop(0, NY, reorder_band, 0)

    halves[0][0].wait_recv()
    for way in range(2):
        for part in ("near", "first", "last"):
            arrivals[way, part].wait_recv()

    def total(b, carry):
        acc = core_sum(0, b)
        for way in range(2):
            acc = acc + near[way, b].astype(F32) + relayed[way, b].astype(F32)
        red[mine + b] = acc.astype(BF16)
        return carry

    lax.fori_loop(0, HALF, total, 0, unroll=4)
    share = remote(red.at[pl.ds(mine, HALF)], red.at[pl.ds(mine, HALF)], red_s, red_r, me, other)
    share.start()
    pending.append(share.wait_send)
    share.wait_recv()

    pl.semaphore_wait(plane.at[2], 1)

    def block_at(t):
        return jnp.clip(tab[c, t], 0, NB - 1)

    in1[me] = red[block_at(me)]

    def dispatch(i, carry):
        t = owner_at(i)
        out1[t] = red[block_at(t)]
        remote(out1.at[t], in1.at[me], a1_s, a1_r, t, dp).start()
        return carry

    lax.fori_loop(0, NO - 1, dispatch, 0)
    pending.append(pltpu.make_async_copy(out1.at[pl.ds(0, NO - 1)], in1.at[pl.ds(0, NO - 1)], a1_s).wait)
    pltpu.make_async_copy(out1.at[pl.ds(0, NO - 1)], in1.at[pl.ds(0, NO - 1)], a1_r).wait()

    live_rows, live_cols = tab[2 + c, me], tab[4 + c, me]
    in_columns = jnp.where(y < live_cols, 1, 0)
    row_limit = live_rows * 2 * in_columns

    def place(q, carry):
        tile = in1[q].astype(F32)
        keep = lax.broadcasted_iota(I32, (16, LANES), 0) < row_limit
        g32[pl.ds(q, 16, stride=NO), :] = jnp.where(keep, tile, 0.0)
        return carry

    lax.fori_loop(0, NO, place, 0, unroll=4)
    masked = g32[pl.ds(0, 8 * LANES), :].astype(BF16)

    my_tile = pl.ds(pl.multiple_of(y * LANES, LANES), LANES)

    def half_band(t, half):
        rows_of_band = lv[pl.ds(pl.multiple_of(t * LANES + half * NO, NO), NO), :]
        return jnp.dot(rows_of_band, masked, preferred_element_type=F32).astype(BF16)

    def send_half(half):
        at = pl.ds(half * NO, NO)
        copies = []
        for i, offset in enumerate(FAR_FIRST):
            t = dp_at(offset)
            prod[half, i] = half_band(t, half)
            copy = remote(
                prod.at[half, i], pin.at[at, my_tile], e_s.at[half, i], e_r.at[half, i], me, t * 2 + c
            )
            copy.start()
            pending.append(copy.wait_send)
            copies.append(copy)
        pin[at, my_tile] = half_band(y, half)
        return copies

    sent = (send_half(0), send_half(1))
    load_r.wait()
    column_limit = live_cols * LANES * jnp.where(y < live_rows, 1, 0)
    keep = lax.broadcasted_iota(I32, (NO, 8 * LANES), 1) < column_limit

    for half in range(2):
        for copy in sent[half]:
            copy.wait_recv()
        update = jnp.dot(pin[half * NO : (half + 1) * NO, :], rv[...], preferred_element_type=F32)
        update = jnp.where(keep, update, 0.0).astype(BF16)
        for to in range(2):
            for j in range(8):
                dsc[half, to, j] = update[to * 32 : (to + 1) * 32, j * LANES : (j + 1) * LANES]
        swap = remote(dsc.at[half, 1 - c], xin.at[half], x_s.at[half], x_r.at[half], me, other)
        swap.start()
        pending.append(swap.wait_send)
        for j in range(8):
            y32[half, pl.ds(c * 8 + j, 32, stride=16), :] = dsc[half, c, j].astype(F32)
        swap.wait_recv()
        for j in range(8):
            y32[half, pl.ds((1 - c) * 8 + j, 32, stride=16), :] = xin[half, j].astype(F32)
        out2[half * 32 : (half + 1) * 32] = y32[half, pl.ds(0, 32 * 16), :].astype(BF16).reshape(32, 16, LANES)

        odd = lax.rem(z + half, 2)

        def give_back(i, carry, half=half, odd=odd):
            u, v = lax.rem(i, 8), lax.div(i, 8)
            there = lax.rem(x + far_first(u), 8)
            depth = lax.rem(z + 4 + lax.div(v + 1, 2) * 2 * (1 - 2 * lax.rem(v, 2)) + 7 * odd, 8)
            at = half * 32 + there * 4 + lax.div(depth, 2)
            remote(out2.at[at], in2.at[me], a2_s, a2_r, there * 8 + depth, dp).start()
            return carry

        lax.fori_loop(0, 31, give_back, 0)

        @pl.when(odd == 1)
        def _(give_back=give_back):
            give_back(31, 0)

        @pl.when(odd == 0)
        def _(half=half):
            in2[me] = out2[half * 32 + lax.div(me, 2)]

    pending.append(pltpu.make_async_copy(out2.at[pl.ds(0, NO - 1)], in2.at[pl.ds(0, NO - 1)], a2_s).wait)
    pltpu.make_async_copy(out2.at[pl.ds(0, NO - 1)], in2.at[pl.ds(0, NO - 1)], a2_r).wait()

    def pick(b, carry):
        both = in2[jnp.clip(tab[6, b], 0, NO - 1)].astype(F32)
        first = jnp.where(tab[7, b] == 0, 1, 0)
        chosen = jnp.where(first == 1, both[:8], both[8:])
        f32s[pl.ds(pl.multiple_of(b * 8, 8), 8), :] = chosen
        return carry

    lax.fori_loop(0, NB, pick, 0, unroll=8)
    for j in range(8):
        out_ref[:, j * LANES : (j + 1) * LANES] = f32s[pl.ds(j, NB, stride=8), :].astype(BF16)

    for wait in pending:
        wait()


def on_device(grads, owner_map, block_dims, left_root, right_root):
    any_spec = pl.BlockSpec(memory_space=pltpu.HBM)
    vmem_spec = pl.BlockSpec(memory_space=pltpu.VMEM)
    dma = pltpu.SemaphoreType.DMA
    out = pl.pallas_call(
        kernel,
        out_shape=jax.ShapeDtypeStruct((NB, 8 * LANES), BF16),
        in_specs=[any_spec, vmem_spec, vmem_spec, any_spec, any_spec],
        out_specs=vmem_spec,
        scratch_shapes=[
            pltpu.VMEM((HALF, 16, 8 * LANES), BF16),
            pltpu.VMEM((8, HALF, 16, LANES), BF16),
            pltpu.VMEM((8, HALF, 16, LANES), BF16),
            pltpu.VMEM((2, QUARTER, 16, LANES), BF16),
            pltpu.VMEM((2, HALF, 16, LANES), BF16),
            pltpu.VMEM((2, HALF, 16, LANES), BF16),
            pltpu.VMEM((2, HALF, 16, LANES), BF16),
            pltpu.VMEM((NB, 16, LANES), BF16),
            pltpu.VMEM((NO, 16, LANES), BF16),
            pltpu.VMEM((NO, 16, LANES), BF16),
            pltpu.VMEM((8 * LANES, 8 * LANES), BF16),
            pltpu.VMEM((8 * LANES, 8 * LANES), BF16),
            pltpu.VMEM((8 * LANES + NO, LANES), F32),
            pltpu.VMEM((2, NY - 1, NO, LANES), BF16),
            pltpu.VMEM((LANES, 8 * LANES), BF16),
            pltpu.VMEM((2, 2, 8, 32, LANES), BF16),
            pltpu.VMEM((2, 8, 32, LANES), BF16),
            pltpu.VMEM((2, 32 * 16 + 16, LANES), F32),
            pltpu.VMEM((NO, 16, LANES), BF16),
            pltpu.VMEM((NO, 16, LANES), BF16),
            pltpu.VMEM((NB * 8 + 8, LANES), F32),
            pltpu.VMEM((8, LANES), I32),
            pltpu.VMEM((8, LANES), I32),
            pltpu.SMEM((8, LANES), I32),
            dma((4,)),
            pltpu.SemaphoreType.REGULAR((3,)),
            dma((8,)), dma((8,)),
            dma((12,)), dma((12,)),
            dma, dma,
            dma, dma,
            dma((2, 7)), dma((2, 7)),
            dma((2,)), dma((2,)),
            dma, dma,
        ],
        compiler_params=pltpu.CompilerParams(
            collective_id=0, has_side_effects=True, vmem_limit_bytes=60 * 1024 * 1024
        ),
    )(
        grads.reshape(NB, 16, 8 * LANES),
        owner_map.reshape(1, NB),
        block_dims.T,
        left_root[0],
        right_root[0],
    )
    return out.reshape(NB, 1, 1, 8 * LANES)


def solution(mesh):
    placed = (
        P("dp", None, None, "owner", None),
        P(),
        P(),
        P("owner", None, None, None),
        P("owner", None, None, None),
    )
    return jax.shard_map(
        on_device,
        mesh=mesh,
        in_specs=placed,
        out_specs=P(None, "dp", "owner", None),
        check_vma=False,
    )
```

```python
import functools

import jax
import jax.numpy as jnp
from jax import lax
from jax.experimental import pallas as pl
from jax.experimental.pallas import tpu as pltpu
from jax.sharding import PartitionSpec as P

MESH = pl.DeviceIdType.MESH
F32, BF16, I32 = jnp.float32, jnp.bfloat16, jnp.int32
NB = 48
HALF = NB // 2
QUARTER = HALF // 2
NO = 64
NY = 8
LANES = 128
FAR_FIRST = (4, 3, 5, 2, 6, 1, 7)
TILE_ORDER = (3, 5, 4, 1, 7, 2, 6, 0)


def remote(src, dst, send_sem, recv_sem, owner, dp):
    return pltpu.make_async_remote_copy(
        src_ref=src, dst_ref=dst, send_sem=send_sem, recv_sem=recv_sem,
        device_id={"owner": owner, "dp": dp}, device_id_type=MESH,
    )


def signal(sem, owner, dp):
    pl.semaphore_signal(sem, inc=1, device_id={"owner": owner, "dp": dp}, device_id_type=MESH)


def diagonal_column(row):
    sub = lax.broadcasted_iota(I32, (LANES, LANES), 0)
    lane = lax.broadcasted_iota(I32, (LANES, LANES), 1)
    return jnp.sum(jnp.where(sub == lane, row, 0), axis=1, keepdims=True)


def build_tables(map_ref, dims_ref, rows, table):
    rows[...] = jnp.full((8, LANES), -1, I32)
    rows[0:1, 0:NB] = map_ref[...]
    rows[1:3, 0:NB] = dims_ref[...]
    sub = lax.broadcasted_iota(I32, (LANES, LANES), 0)
    lane = lax.broadcasted_iota(I32, (LANES, LANES), 1)
    owner_row = rows[0:1, :]
    owner_col = diagonal_column(owner_row)
    live_rows = diagonal_column(rows[1:2, :])
    live_cols = diagonal_column(rows[2:3, :])
    same = owner_col == owner_row
    slot_row = jnp.sum(jnp.where(same & (sub < lane), 1, 0), axis=0, keepdims=True)
    slot_col = jnp.sum(jnp.where(same & (lane < sub), 1, 0), axis=1, keepdims=True)
    owned = owner_col == lane
    for slot in range(2):
        hit = owned & (slot_col == slot)
        for row, value in ((slot, sub), (2 + slot, live_rows), (4 + slot, live_cols)):
            table[row : row + 1, :] = jnp.sum(jnp.where(hit, value, 0), axis=0, keepdims=True)
    table[6:7, :] = owner_row
    table[7:8, :] = slot_row


def kernel(
    grads, map_ref, dims_ref, left, right, out_ref,
    g, gin, pair, far, mid, near, relayed, red, out1, in1, lv, rv, g32, prod, pin, dsc, xin, y32, out2, in2, f32s, rows, table, tab,
    load_sem, plane, core_s, core_r, rs_s, rs_r, red_s, red_r, a1_s, a1_r, e_s, e_r, x_s, x_r, a2_s, a2_r,
):
    me = lax.axis_index("owner")
    dp = lax.axis_index("dp")
    x, z = lax.div(me, 8), lax.rem(me, 8)
    y, c = lax.div(dp, 2), lax.rem(dp, 2)
    other = dp + 1 - 2 * c

    load_g = pltpu.make_async_copy(grads, g, load_sem.at[0])
    load_l = pltpu.make_async_copy(left.at[c], lv, load_sem.at[1])
    load_r = pltpu.make_async_copy(right.at[c], rv, load_sem.at[2])
    load_g.start()

    def in_line(i):
        return lax.rem(x + i * c, 8) * 8 + lax.rem(z + i * (1 - c), 8)

    def far_first(i):
        return 4 + lax.div(i + 1, 2) * (1 - 2 * lax.rem(i, 2))

    def owner_at(i):
        return lax.rem(x + far_first(lax.rem(i, 8)), 8) * 8 + lax.rem(z + far_first(lax.div(i, 8)), 8)

    def dp_at(offset):
        return lax.rem(y + offset, NY)

    pending = []
    barrier = pltpu.get_barrier_semaphore()
    signal(barrier, me, other)
    for offset in (1, 7, 2, 6):
        signal(barrier, me, dp_at(offset) * 2 + c)
    for i in range(1, 8):
        signal(barrier, in_line(i), dp)
    pl.semaphore_wait(barrier, 1 + 4 + 7)

    mine, theirs = c * HALF, (1 - c) * HALF
    load_g.wait()
    halves = {}
    for offset in TILE_ORDER:
        tile = pl.ds(pl.multiple_of(dp_at(offset) * LANES, LANES), LANES)
        copy = remote(
            g.at[pl.ds(theirs, HALF), :, tile], gin.at[offset], core_s.at[offset], core_r.at[offset], me, other
        )
        copy.start()
        pending.append(copy.wait_send)
        halves[offset] = (copy, tile)
    load_l.start()
    load_r.start()
    signal(plane.at[0], me, other)

    def core_sum(offset, b):
        return g[mine + b, :, halves[offset][1]].astype(F32) + gin[offset, b].astype(F32)

    def sum_blocks(offset, first, count, terms=()):
        def add(b, carry):
            acc = core_sum(offset, first + b)
            for buffer, way, start in terms:
                acc = acc + buffer[way, start + b].astype(F32)
            pair[offset, first + b] = acc.astype(BF16)
            return carry

        lax.fori_loop(0, count, add, 0, unroll=4)

    def send_sums(offset, first, count, target, buffer, k):
        copy = remote(
            pair.at[offset, pl.ds(first, count)], buffer, rs_s.at[k], rs_r.at[k], me, dp_at(target) * 2 + c
        )
        copy.start()
        pending.append(copy.wait_send)
        return copy

    ways = ((0, 2, 3, 1, 0, QUARTER), (1, 6, 5, 7, QUARTER, 0))
    arrivals = {}
    for way, own, three, step, both, alone in ways:
        halves[three][0].wait_recv()
        sum_blocks(three, alone, QUARTER)
        arrivals[way, "alone"] = send_sums(three, alone, QUARTER, step, mid.at[way, pl.ds(alone, QUARTER)], way)
    halves[4][0].wait_recv()
    for way, own, three, step, both, alone in ways:
        sum_blocks(4, both, QUARTER)
        arrivals[way, "far"] = send_sums(4, both, QUARTER, own, far.at[way], 2 + way)
    for way, own, three, step, both, alone in ways:
        sum_blocks(three, both, QUARTER)
        arrivals[way, "both"] = send_sums(three, both, QUARTER, step, mid.at[way, pl.ds(both, QUARTER)], 4 + way)
    for way, own, three, step, both, alone in ways:
        halves[step][0].wait_recv()
        sum_blocks(step, 0, HALF)
        arrivals[way, "near"] = send_sums(step, 0, HALF, step, near.at[way], 6 + way)
    pl.semaphore_wait(plane.at[0], 1)
    for i in range(1, 8):
        signal(plane.at[1], in_line(i), dp)
    for way, own, three, step, both, alone in ways:
        halves[own][0].wait_recv()
        arrivals[way, "alone"].wait_recv()
        sum_blocks(own, alone, QUARTER, ((mid, way, alone),))
        arrivals[way, "first"] = send_sums(own, alone, QUARTER, own, relayed.at[way, pl.ds(alone, QUARTER)], 8 + way)
    for way, own, three, step, both, alone in ways:
        arrivals[way, "far"].wait_recv()
        arrivals[way, "both"].wait_recv()
        sum_blocks(own, both, QUARTER, ((mid, way, both), (far, way, 0)))
        arrivals[way, "last"] = send_sums(own, both, QUARTER, own, relayed.at[way, pl.ds(both, QUARTER)], 10 + way)

    pl.semaphore_wait(plane.at[1], 7)
    signal(plane.at[2], me, other)
    build_tables(map_ref, dims_ref, rows, table)
    to_scalars = pltpu.make_async_copy(table, tab, load_sem.at[3])
    to_scalars.start()
    to_scalars.wait()

    load_l.wait()
    new_row = lax.broadcasted_iota(I32, (LANES, LANES), 0)
    old_row = (new_row // 32) % 2 * NO + new_row % 32 * 2 + new_row // NO
    reorder = jnp.where(lax.broadcasted_iota(I32, (LANES, LANES), 1) == old_row, 1.0, 0.0).astype(BF16)

    def reorder_band(t, carry):
        at = pl.ds(pl.multiple_of(t * LANES, LANES), LANES)
        lv[at, :] = jnp.dot(reorder, lv[at, :], preferred_element_type=F32).astype(BF16)
        return carry

    lax.fori_loop(0, NY, reorder_band, 0)

    halves[0][0].wait_recv()
    for way in range(2):
        for part in ("near", "first", "last"):
            arrivals[way, part].wait_recv()

    def total(b, carry):
        acc = core_sum(0, b)
        for way in range(2):
            acc = acc + near[way, b].astype(F32) + relayed[way, b].astype(F32)
        red[mine + b] = acc.astype(BF16)
        return carry

    lax.fori_loop(0, HALF, total, 0, unroll=4)
    share = remote(red.at[pl.ds(mine, HALF)], red.at[pl.ds(mine, HALF)], red_s, red_r, me, other)
    share.start()
    pending.append(share.wait_send)
    share.wait_recv()

    pl.semaphore_wait(plane.at[2], 1)

    def block_at(t):
        return jnp.clip(tab[c, t], 0, NB - 1)

    in1[me] = red[block_at(me)]

    def dispatch(i, carry):
        t = owner_at(i)
        out1[t] = red[block_at(t)]
        remote(out1.at[t], in1.at[me], a1_s, a1_r, t, dp).start()
        return carry

    lax.fori_loop(0, NO - 1, dispatch, 0)
    pending.append(pltpu.make_async_copy(out1.at[pl.ds(0, NO - 1)], in1.at[pl.ds(0, NO - 1)], a1_s).wait)
    pltpu.make_async_copy(out1.at[pl.ds(0, NO - 1)], in1.at[pl.ds(0, NO - 1)], a1_r).wait()

    live_rows, live_cols = tab[2 + c, me], tab[4 + c, me]
    in_columns = jnp.where(y < live_cols, 1, 0)
    row_limit = live_rows * 2 * in_columns

    def place(q, carry):
        tile = in1[q].astype(F32)
        keep = lax.broadcasted_iota(I32, (16, LANES), 0) < row_limit
        g32[pl.ds(q, 16, stride=NO), :] = jnp.where(keep, tile, 0.0)
        return carry

    lax.fori_loop(0, NO, place, 0, unroll=4)
    masked = g32[pl.ds(0, 8 * LANES), :].astype(BF16)

    my_tile = pl.ds(pl.multiple_of(y * LANES, LANES), LANES)

    def half_band(t, half):
        rows_of_band = lv[pl.ds(pl.multiple_of(t * LANES + half * NO, NO), NO), :]
        return jnp.dot(rows_of_band, masked, preferred_element_type=F32).astype(BF16)

    def send_half(half):
        at = pl.ds(half * NO, NO)
        copies = []
        for i, offset in enumerate(FAR_FIRST):
            t = dp_at(offset)
            prod[half, i] = half_band(t, half)
            copy = remote(
                prod.at[half, i], pin.at[at, my_tile], e_s.at[half, i], e_r.at[half, i], me, t * 2 + c
            )
            copy.start()
            pending.append(copy.wait_send)
            copies.append(copy)
        pin[at, my_tile] = half_band(y, half)
        return copies

    sent = (send_half(0), send_half(1))
    load_r.wait()
    column_limit = live_cols * LANES * jnp.where(y < live_rows, 1, 0)
    keep = lax.broadcasted_iota(I32, (NO, 8 * LANES), 1) < column_limit

    for half in range(2):
        for copy in sent[half]:
            copy.wait_recv()
        update = jnp.dot(pin[half * NO : (half + 1) * NO, :], rv[...], preferred_element_type=F32)
        update = jnp.where(keep, update, 0.0).astype(BF16)
        for to in range(2):
            for j in range(8):
                dsc[half, to, j] = update[to * 32 : (to + 1) * 32, j * LANES : (j + 1) * LANES]
        swap = remote(dsc.at[half, 1 - c], xin.at[half], x_s.at[half], x_r.at[half], me, other)
        swap.start()
        pending.append(swap.wait_send)
        for j in range(8):
            y32[half, pl.ds(c * 8 + j, 32, stride=16), :] = dsc[half, c, j].astype(F32)
        swap.wait_recv()
        for j in range(8):
            y32[half, pl.ds((1 - c) * 8 + j, 32, stride=16), :] = xin[half, j].astype(F32)
        out2[half * 32 : (half + 1) * 32] = y32[half, pl.ds(0, 32 * 16), :].astype(BF16).reshape(32, 16, LANES)

        odd = lax.rem(z + half, 2)

        def give_back(i, carry, half=half, odd=odd):
            u, v = lax.rem(i, 8), lax.div(i, 8)
            there = lax.rem(x + far_first(u), 8)
            depth = lax.rem(z + 4 + lax.div(v + 1, 2) * 2 * (1 - 2 * lax.rem(v, 2)) + 7 * odd, 8)
            at = half * 32 + there * 4 + lax.div(depth, 2)
            remote(out2.at[at], in2.at[me], a2_s, a2_r, there * 8 + depth, dp).start()
            return carry

        lax.fori_loop(0, 31, give_back, 0)

        @pl.when(odd == 1)
        def _(give_back=give_back):
            give_back(31, 0)

        @pl.when(odd == 0)
        def _(half=half):
            in2[me] = out2[half * 32 + lax.div(me, 2)]

    pending.append(pltpu.make_async_copy(out2.at[pl.ds(0, NO - 1)], in2.at[pl.ds(0, NO - 1)], a2_s).wait)
    pltpu.make_async_copy(out2.at[pl.ds(0, NO - 1)], in2.at[pl.ds(0, NO - 1)], a2_r).wait()

    def pick(b, carry):
        both = in2[jnp.clip(tab[6, b], 0, NO - 1)].astype(F32)
        first = jnp.where(tab[7, b] == 0, 1, 0)
        chosen = jnp.where(first == 1, both[:8], both[8:])
        f32s[pl.ds(pl.multiple_of(b * 8, 8), 8), :] = chosen
        return carry

    lax.fori_loop(0, NB, pick, 0, unroll=8)
    for j in range(8):
        out_ref[:, j * LANES : (j + 1) * LANES] = f32s[pl.ds(j, NB, stride=8), :].astype(BF16)

    for wait in pending:
        wait()


def on_device(grads, owner_map, block_dims, left_root, right_root):
    any_spec = pl.BlockSpec(memory_space=pltpu.HBM)
    vmem_spec = pl.BlockSpec(memory_space=pltpu.VMEM)
    dma = pltpu.SemaphoreType.DMA
    out = pl.pallas_call(
        kernel,
        out_shape=jax.ShapeDtypeStruct((NB, 8 * LANES), BF16),
        in_specs=[any_spec, vmem_spec, vmem_spec, any_spec, any_spec],
        out_specs=vmem_spec,
        scratch_shapes=[
            pltpu.VMEM((NB, 16, 8 * LANES), BF16),
            pltpu.VMEM((8, HALF, 16, LANES), BF16),
            pltpu.VMEM((8, HALF, 16, LANES), BF16),
            pltpu.VMEM((2, QUARTER, 16, LANES), BF16),
            pltpu.VMEM((2, HALF, 16, LANES), BF16),
            pltpu.VMEM((2, HALF, 16, LANES), BF16),
            pltpu.VMEM((2, HALF, 16, LANES), BF16),
            pltpu.VMEM((NB, 16, LANES), BF16),
            pltpu.VMEM((NO, 16, LANES), BF16),
            pltpu.VMEM((NO, 16, LANES), BF16),
            pltpu.VMEM((8 * LANES, 8 * LANES), BF16),
            pltpu.VMEM((8 * LANES, 8 * LANES), BF16),
            pltpu.VMEM((8 * LANES + NO, LANES), F32),
            pltpu.VMEM((2, NY - 1, NO, LANES), BF16),
            pltpu.VMEM((LANES, 8 * LANES), BF16),
            pltpu.VMEM((2, 2, 8, 32, LANES), BF16),
            pltpu.VMEM((2, 8, 32, LANES), BF16),
            pltpu.VMEM((2, 32 * 16 + 16, LANES), F32),
            pltpu.VMEM((NO, 16, LANES), BF16),
            pltpu.VMEM((NO, 16, LANES), BF16),
            pltpu.VMEM((NB * 8 + 8, LANES), F32),
            pltpu.VMEM((8, LANES), I32),
            pltpu.VMEM((8, LANES), I32),
            pltpu.SMEM((8, LANES), I32),
            dma((4,)),
            pltpu.SemaphoreType.REGULAR((3,)),
            dma((8,)), dma((8,)),
            dma((12,)), dma((12,)),
            dma, dma,
            dma, dma,
            dma((2, 7)), dma((2, 7)),
            dma((2,)), dma((2,)),
            dma, dma,
        ],
        compiler_params=pltpu.CompilerParams(
            collective_id=0, has_side_effects=True, vmem_limit_bytes=60 * 1024 * 1024
        ),
    )(
        grads.reshape(NB, 16, 8 * LANES),
        owner_map.reshape(1, NB),
        block_dims.T,
        left_root[0],
        right_root[0],
    )
    return out.reshape(NB, 1, 1, 8 * LANES)


def solution(mesh):
    placed = (
        P("dp", None, None, "owner", None),
        P(),
        P(),
        P("owner", None, None, None),
        P("owner", None, None, None),
    )
    return jax.shard_map(
        on_device,
        mesh=mesh,
        in_specs=placed,
        out_specs=P(None, "dp", "owner", None),
        check_vma=False,
    )
```
